128 devices in a mesh: cells: 16 (over z, x), sub: 8 (over y, core).
Axes of the slice: x: 4, y: 4, z: 4, core: 2. Of those that a mesh axis runs over, the one named last changes fastest.
Arguments:
- send_cells: int32 [128, 128, 1], P(('cells', 'sub')), may hold values from -1 to 15, as said below
- pair_cell: int32 [128, 128, 1], P(('cells', 'sub')), may hold values from 0 to 15
- counts: int32 [2048], P(('cells', 'sub')), may hold values from 1 to 128, as said below
- positions: float32 [3, 2048, 128], P(None, ('cells', 'sub')), may hold values from 0 to 1.5, as said below
- mass: float32 [2048, 128], P(('cells', 'sub')), may hold values from 0.004 to 0.016
- smooth: float32 [2048, 128], P(('cells', 'sub')), may hold values from 0.5 to 1
- entropy: float32 [2048, 128], P(('cells', 'sub')), may hold values from 0.5 to 2
Outputs:
- density: float32 [2048, 128], P(('cells', 'sub'))
- accel: float32 [3, 2048, 128], P(None, ('cells', 'sub'))
The draws below stay inside these ranges and needn't reach their ends.
Inputs may be any that keep to these rules, and one draw needn't show every extreme that they name: send_cells[p, q, k] is the index within device p of a cell that p pairs with device q, or -1 for an empty slot; the cells that p names for one q are distinct; send_cells[p, p, k] = -1. `counts`: slots of a cell at or above its count are padding; whole devices differ in their cells' occupancy. `positions`: each cell's particles lie in a unit cube of its own, whose corner lies in [0, 0.5] along each component.
All inputs are finite; a program needn't handle non-finite values.
Results may differ from the reference program's by a relative error of at most 0.00016.
Values sent between devices are 32-bit elements; how exact they have to be, the bound alone decides.
A program may use at most 64 MiB of HBM per device.

```python
import math
import jax
import jax.numpy as jnp
from jax import lax

SLOTS = 128
CELL_DEV = 16
CAP = 1
CELLS = 2048
DEVICES = 128


def draw_send_cells(key, part):
    key = jax.random.fold_in(key, 11)
    first_key, stride_key, use_key = jax.random.split(key, 3)
    first = jax.random.randint(first_key, (DEVICES, DEVICES, 1), 0, CELL_DEV)
    stride = jax.random.randint(stride_key, (DEVICES, DEVICES, 1), 1, CELL_DEV // CAP + 1)
    chosen = (first + stride * jnp.arange(CAP)[None, None, :]) % CELL_DEV
    in_use = jax.random.randint(use_key, (DEVICES, DEVICES, CAP), 0, 5) < 3
    source = jnp.arange(DEVICES)[:, None, None]
    target = jnp.arange(DEVICES)[None, :, None]
    in_use = jnp.logical_and(in_use, source != target)
    chosen = jnp.where(in_use, chosen, -1)
    return chosen.at[0, 1, 0].set(CELL_DEV - 1).astype(jnp.int32)


def draw_counts(key, part):
    key = jax.random.fold_in(key, 23)
    top_key, count_key = jax.random.split(key)
    top = 32 * jax.random.randint(top_key, (DEVICES, 1), 1, 5)
    top = top.at[0, 0].set(SLOTS)
    filled = jax.random.randint(count_key, (DEVICES, CELL_DEV), 1, top + 1)
    filled = filled.at[0, 0].set(SLOTS)
    return filled.reshape(DEVICES * CELL_DEV).astype(jnp.int32)


def draw_positions(key, part):
    key = jax.random.fold_in(key, 37)
    corner_key, inner_key = jax.random.split(key)
    corner = jax.random.uniform(corner_key, (3, CELLS, 1), jnp.float32, 0.0, 0.5)
    inner = jax.random.uniform(inner_key, (3, CELLS, SLOTS), jnp.float32, 0.0, 1.0)
    return (corner + inner).astype(jnp.float32)


def touch_ends(values, rng, least, high):
    shape = values.shape
    index_at = [jax.random.randint(jax.random.fold_in(rng, axis), (), 0, shape[axis]) for axis in range(len(shape))]
    values = values.at[tuple(index_at)].set(least)
    longest = shape.index(max(shape))
    index_at[longest] = (index_at[longest] + 1) % shape[longest]
    return values.at[tuple(index_at)].set(high)


def block_scale(own_key, shape, shards, smallest, high):
    factor_of = 1.0
    for dim, parts in shards:
        steps = jax.random.uniform(jax.random.fold_in(jax.random.fold_in(own_key, 6), dim), (parts,), jnp.float32, smallest / len(shards), high / len(shards))
        factor_of = factor_of * jnp.repeat(jnp.exp(steps), shape[dim] // parts).reshape((-1,) + (1,) * (len(shape) - 1 - dim))
    return factor_of


def setup_inputs(seed: int = 0) -> dict:
    key_of = jax.random.split(jax.random.key(seed), 8)
    send_cells = draw_send_cells(jax.random.fold_in(key_of[7], 71), 0)
    pair_cell = touch_ends(jax.random.randint(key_of[1], (DEVICES, DEVICES, CAP), 0, CELL_DEV), jax.random.fold_in(key_of[1], 1), 0, CELL_DEV - 1).astype(jnp.int32)
    counts = draw_counts(jax.random.fold_in(key_of[7], 71), 0)
    positions = draw_positions(jax.random.fold_in(key_of[7], 71), 0)
    mass = jnp.clip(jnp.exp(math.log(0.016) - 1.3862944 * jax.random.uniform(key_of[4], (CELLS, SLOTS), jnp.float32) ** block_scale(key_of[4], (CELLS, SLOTS), ((0, 128),), -0.2, 0.2)), 0.004, 0.016)
    smooth = jnp.clip(0.5 + 0.5 * jax.random.uniform(key_of[5], (CELLS, SLOTS), jnp.float32) ** block_scale(key_of[5], (CELLS, SLOTS), ((0, 128),), -0.2, 0.2), 0.5, 1.0)
    entropy = jnp.clip(jnp.exp(math.log(2.0) - 1.3862944 * jax.random.uniform(key_of[6], (CELLS, SLOTS), jnp.float32) ** block_scale(key_of[6], (CELLS, SLOTS), ((0, 128),), -0.2, 0.2)), 0.5, 2.0)
    return dict(send_cells=send_cells, pair_cell=pair_cell, counts=counts, positions=positions, mass=mass, smooth=smooth, entropy=entropy)


KERNEL_NORM = 21.0 / (2.0 * math.pi)

def kernel_weight(dist_sq, smooth_len):
    scaled = jnp.sqrt(dist_sq) / smooth_len
    inside = jnp.maximum(1.0 - scaled, 0.0)
    cube = smooth_len * smooth_len * smooth_len
    return KERNEL_NORM / cube * inside * inside * inside * inside * (1.0 + 4.0 * scaled)

def kernel_slope(dist_sq, smooth_len):
    scaled = jnp.sqrt(dist_sq) / smooth_len
    inside = jnp.maximum(1.0 - scaled, 0.0)
    fifth = smooth_len * smooth_len * smooth_len * smooth_len * smooth_len
    return -20.0 * KERNEL_NORM / fifth * inside * inside * inside

def density_tile(pos_a, len_a, mass_a, pos_b, len_b, mass_b):
    offset = pos_a[..., :, None] - pos_b[..., None, :]
    dist_sq = lax.optimization_barrier(jnp.sum(offset * offset, axis=0))
    to_a = lax.optimization_barrier(jnp.sum(kernel_weight(dist_sq, len_a[..., :, None]) * mass_b[..., None, :], axis=-1))
    to_b = lax.optimization_barrier(jnp.sum(kernel_weight(dist_sq, len_b[..., None, :]) * mass_a[..., :, None], axis=-2))
    return (to_a, to_b)

def force_tile(pos_a, len_a, mass_a, press_a, pos_b, len_b, mass_b, press_b):
    offset = pos_a[..., :, None] - pos_b[..., None, :]
    dist_sq = lax.optimization_barrier(jnp.sum(offset * offset, axis=0))
    strength = press_a[..., :, None] * kernel_slope(dist_sq, len_a[..., :, None]) + press_b[..., None, :] * kernel_slope(dist_sq, len_b[..., None, :])
    to_a = -lax.optimization_barrier(jnp.sum(offset * (strength * mass_b[..., None, :])[None], axis=-1))
    to_b = lax.optimization_barrier(jnp.sum(offset * (strength * mass_a[..., :, None])[None], axis=-2))
    return (to_a, to_b)

def local_density(pos, lens, mass):
    cell_count = mass.shape[0]
    has_next = (jnp.arange(cell_count) < cell_count - 1).astype(jnp.float32)[:, None]
    own_part, unused = density_tile(pos, lens, mass, pos, lens, mass)
    next_mass = jnp.roll(mass, -1, axis=0) * has_next
    to_here, to_next = density_tile(pos, lens, mass, jnp.roll(pos, -1, axis=1), jnp.roll(lens, -1, axis=0), next_mass)
    return own_part + to_here + jnp.roll(to_next * has_next, 1, axis=0)

def local_force(pos, lens, mass, pressure):
    cell_count = mass.shape[0]
    has_next = (jnp.arange(cell_count) < cell_count - 1).astype(jnp.float32)[:, None]
    own_part, unused = force_tile(pos, lens, mass, pressure, pos, lens, mass, pressure)
    next_mass = jnp.roll(mass, -1, axis=0) * has_next
    to_here, to_next = force_tile(pos, lens, mass, pressure, jnp.roll(pos, -1, axis=1), jnp.roll(lens, -1, axis=0), next_mass, jnp.roll(pressure, -1, axis=0))
    return own_part + to_here + jnp.roll(to_next * has_next[None], 1, axis=1)

def reference(send_cells, pair_cell, counts, positions, mass, smooth, entropy):
    occupied = jnp.arange(SLOTS)[None, :] < counts[:, None]
    mass_eff = jnp.where(occupied, mass, 0.0)
    dev_pos = positions.reshape(3, DEVICES, CELL_DEV, SLOTS).transpose(1, 0, 2, 3)
    dev_len = smooth.reshape(DEVICES, CELL_DEV, SLOTS)
    dev_mass = mass_eff.reshape(DEVICES, CELL_DEV, SLOTS)

    def local_step(items):
        return local_density(items[0], items[1], items[2])
    local_rho = lax.map(local_step, (dev_pos, dev_len, dev_mass)).reshape(CELLS, SLOTS)
    source = jnp.arange(DEVICES)[:, None, None]
    target = jnp.arange(DEVICES)[None, :, None]
    far_cell = (source * CELL_DEV + jnp.maximum(send_cells, 0)).astype(jnp.int32).reshape(-1, 64)
    near_cell = (target * CELL_DEV + jnp.transpose(pair_cell, (1, 0, 2))).astype(jnp.int32).reshape(-1, 64)
    alive_flag = (send_cells >= 0).astype(jnp.float32).reshape(-1, 64)

    def density_pairs(accumulated, items):
        idx_far, idx_near, alive = items
        far_mass = mass_eff[idx_far] * alive[:, None]
        to_near, to_far = density_tile(positions[:, idx_near], smooth[idx_near], mass_eff[idx_near], positions[:, idx_far], smooth[idx_far], far_mass)
        accumulated = accumulated.at[idx_near].add(to_near)
        accumulated = accumulated.at[idx_far].add(to_far * alive[:, None])
        return (accumulated, None)
    foreign_rho, unused = lax.scan(density_pairs, jnp.zeros((CELLS, SLOTS), jnp.float32), (far_cell, near_cell, alive_flag))
    total = local_rho + foreign_rho
    density = jnp.where(occupied, total, 0.0)
    pressure = jnp.where(occupied, entropy * jnp.power(jnp.where(occupied, total, 1.0), -1.0 / 3.0), 0.0)
    dev_press = pressure.reshape(DEVICES, CELL_DEV, SLOTS)

    def local_force_step(items):
        return local_force(items[0], items[1], items[2], items[3])
    local_acc = lax.map(local_force_step, (dev_pos, dev_len, dev_mass, dev_press))
    local_acc = local_acc.transpose(1, 0, 2, 3).reshape(3, CELLS, SLOTS)

    def force_pairs(accumulated, items):
        idx_far, idx_near, alive = items
        far_mass = mass_eff[idx_far] * alive[:, None]
        to_near, to_far = force_tile(positions[:, idx_near], smooth[idx_near], mass_eff[idx_near], pressure[idx_near], positions[:, idx_far], smooth[idx_far], far_mass, pressure[idx_far])
        accumulated = accumulated.at[:, idx_near].add(to_near)
        accumulated = accumulated.at[:, idx_far].add(to_far * alive[None, :, None])
        return (accumulated, None)
    foreign_acc, unused = lax.scan(force_pairs, jnp.zeros((3, CELLS, SLOTS), jnp.float32), (far_cell, near_cell, alive_flag))
    accel = jnp.where(occupied[None], local_acc + foreign_acc, 0.0)
    return (density, accel)
```

```python
import functools
import math

import jax
import jax.numpy as jnp
from jax import lax
from jax.experimental import pallas as pl
from jax.experimental.pallas import tpu as pltpu
from jax.sharding import PartitionSpec as P

KERNEL_NORM = 21.0 / (2.0 * math.pi)


def kernel_weight(dist_sq, smooth_len):
    scaled = jnp.sqrt(dist_sq) / smooth_len
    inside = jnp.maximum(1.0 - scaled, 0.0)
    cube = smooth_len * smooth_len * smooth_len
    return KERNEL_NORM / cube * inside * inside * inside * inside * (1.0 + 4.0 * scaled)


def kernel_slope(dist_sq, smooth_len):
    scaled = jnp.sqrt(dist_sq) / smooth_len
    inside = jnp.maximum(1.0 - scaled, 0.0)
    fifth = smooth_len * smooth_len * smooth_len * smooth_len * smooth_len
    return -20.0 * KERNEL_NORM / fifth * inside * inside * inside


def density_tile(pos_a, len_a, mass_a, pos_b, len_b, mass_b):
    offset = pos_a[..., :, None] - pos_b[..., None, :]
    dist_sq = jnp.sum(offset * offset, axis=0)
    to_a = jnp.sum(kernel_weight(dist_sq, len_a[..., :, None]) * mass_b[..., None, :], axis=-1)
    to_b = jnp.sum(kernel_weight(dist_sq, len_b[..., None, :]) * mass_a[..., :, None], axis=-2)
    return (to_a, to_b)


def force_tile(pos_a, len_a, mass_a, press_a, pos_b, len_b, mass_b, press_b):
    offset = pos_a[..., :, None] - pos_b[..., None, :]
    dist_sq = jnp.sum(offset * offset, axis=0)
    strength = press_a[..., :, None] * kernel_slope(dist_sq, len_a[..., :, None]) + press_b[
        ..., None, :
    ] * kernel_slope(dist_sq, len_b[..., None, :])
    to_a = -jnp.sum(offset * (strength * mass_b[..., None, :])[None], axis=-1)
    to_b = jnp.sum(offset * (strength * mass_a[..., :, None])[None], axis=-2)
    return (to_a, to_b)


def local_density(pos, lens, mass):
    cell_count = mass.shape[0]
    has_next = (jnp.arange(cell_count) < cell_count - 1).astype(jnp.float32)[:, None]
    own_part, unused = density_tile(pos, lens, mass, pos, lens, mass)
    next_mass = jnp.roll(mass, -1, axis=0) * has_next
    to_here, to_next = density_tile(
        pos, lens, mass, jnp.roll(pos, -1, axis=1), jnp.roll(lens, -1, axis=0), next_mass
    )
    return own_part + to_here + jnp.roll(to_next * has_next, 1, axis=0)


def local_force(pos, lens, mass, pressure):
    cell_count = mass.shape[0]
    has_next = (jnp.arange(cell_count) < cell_count - 1).astype(jnp.float32)[:, None]
    own_part, unused = force_tile(pos, lens, mass, pressure, pos, lens, mass, pressure)
    next_mass = jnp.roll(mass, -1, axis=0) * has_next
    to_here, to_next = force_tile(
        pos,
        lens,
        mass,
        pressure,
        jnp.roll(pos, -1, axis=1),
        jnp.roll(lens, -1, axis=0),
        next_mass,
        jnp.roll(pressure, -1, axis=0),
    )
    return own_part + to_here + jnp.roll(to_next * has_next[None], 1, axis=1)


def blockwise(tile_fn, arrays, tile_rows):
    total_rows = arrays[1].shape[0]

    def one_tile(turn_index):
        begin_at = turn_index * tile_rows
        pieces = [
            lax.dynamic_slice_in_dim(array, begin_at, tile_rows, array.ndim - 2) for array in arrays
        ]
        return tile_fn(*pieces)

    return lax.map(one_tile, jnp.arange(total_rows // tile_rows))


LOGICAL = pl.DeviceIdType.LOGICAL


def exchange_kernel(ring, peers, x_ref, out_ref, send_sem, recv_sem, ready_sem):
    me = lax.axis_index(("cells", "sub"))
    barrier = pltpu.get_barrier_semaphore()
    for step in range(1, ring):
        pl.semaphore_signal(barrier, inc=1, device_id=me ^ step, device_id_type=LOGICAL)
    for step in range(1, peers // ring):
        pl.semaphore_signal(
            barrier, inc=1, device_id=me ^ (ring * step), device_id_type=LOGICAL
        )
    pl.semaphore_wait(barrier, ring + peers // ring - 2)
    for step in range(1, ring):
        pl.semaphore_signal(ready_sem, inc=1, device_id=me ^ step, device_id_type=LOGICAL)
    pl.semaphore_wait(ready_sem, ring - 1)

    def send(step, carry):
        peer = me ^ step
        pltpu.make_async_remote_copy(
            src_ref=x_ref.at[peer],
            dst_ref=out_ref.at[me],
            send_sem=send_sem,
            recv_sem=recv_sem,
            device_id=peer,
            device_id_type=LOGICAL,
        ).start()
        return carry

    lax.fori_loop(1, peers, send, 0)
    out_ref[pl.ds(me, 1)] = x_ref[pl.ds(me, 1)]
    moved = x_ref.at[pl.ds(0, peers - 1)]
    pltpu.make_async_copy(moved, moved, send_sem).wait()
    landed = out_ref.at[pl.ds(0, peers - 1)]
    pltpu.make_async_copy(landed, landed, recv_sem).wait()


def exchange(x, ring, number):
    peers = x.shape[0]
    return pl.pallas_call(
        functools.partial(exchange_kernel, ring, peers),
        out_shape=jax.ShapeDtypeStruct(x.shape, x.dtype),
        in_specs=[pl.BlockSpec(memory_space=pltpu.VMEM)],
        out_specs=pl.BlockSpec(memory_space=pltpu.VMEM),
        scratch_shapes=[
            pltpu.SemaphoreType.DMA,
            pltpu.SemaphoreType.DMA,
            pltpu.SemaphoreType.REGULAR,
        ],
        compiler_params=pltpu.CompilerParams(
            collective_id=number, has_side_effects=True, vmem_limit_bytes=32 * 2**20
        ),
        name=f"exchange{number}",
    )(x)


def on_device(send_cells, pair_cell, counts, positions, mass, smooth, entropy):
    cell_dev = mass.shape[0]
    slots = mass.shape[1]
    per_peer = send_cells.shape[2]
    peer_count = lax.axis_size(("cells", "sub"))
    ring = lax.axis_size("sub")
    far_rows = peer_count * per_peer
    tile_rows = 16
    occupied = jnp.arange(slots)[None, :] < counts[:, None]
    mass_eff = jnp.where(occupied, mass, 0.0)
    chosen = send_cells[0]
    in_use = (chosen >= 0).astype(jnp.float32)
    picked = jnp.maximum(chosen, 0)
    out_pos = positions[:, picked]
    outgoing = jnp.concatenate(
        [out_pos, smooth[picked][None], (mass_eff[picked] * in_use[..., None])[None]], axis=0
    )
    far_data = exchange(outgoing.reshape(5, far_rows, slots).transpose(1, 0, 2), ring, 0).transpose(1, 0, 2)
    partner = pair_cell[0].reshape(far_rows)
    near_pos = positions[:, partner]
    near_len = smooth[partner]
    near_mass = mass_eff[partner]
    cell_ids = jnp.arange(cell_dev)
    near_owner = (partner[:, None] == cell_ids[None, :]).astype(jnp.float32)
    sent_owner = (picked.reshape(far_rows)[:, None] == cell_ids[None, :]).astype(
        jnp.float32
    ) * in_use.reshape(far_rows)[:, None]
    to_near, to_far = blockwise(
        density_tile,
        (near_pos, near_len, near_mass, far_data[:3], far_data[3], far_data[4]),
        tile_rows,
    )
    to_near = to_near.reshape(far_rows, slots)
    returned = exchange(to_far.reshape(far_rows, 1, slots), ring, 1).reshape(far_rows, slots)
    near_sum = jnp.einsum("rs,rc->cs", to_near, near_owner, precision=lax.Precision.HIGHEST)
    back_sum = jnp.einsum("rs,rc->cs", returned, sent_owner, precision=lax.Precision.HIGHEST)
    total = local_density(positions, smooth, mass_eff) + near_sum + back_sum
    density = jnp.where(occupied, total, 0.0)
    safe_total = jnp.where(occupied, total, 1.0)
    pressure = jnp.where(occupied, entropy * jnp.power(safe_total, -1.0 / 3.0), 0.0)
    far_press = exchange(pressure[picked], ring, 2).reshape(far_rows, slots)
    near_press = pressure[partner]
    acc_near, acc_far = blockwise(
        force_tile,
        (
            near_pos,
            near_len,
            near_mass,
            near_press,
            far_data[:3],
            far_data[3],
            far_data[4],
            far_press,
        ),
        tile_rows,
    )
    acc_near = acc_near.transpose(1, 0, 2, 3).reshape(3, far_rows, slots)
    acc_far = acc_far.transpose(0, 2, 1, 3).reshape(far_rows, 3, slots)
    acc_back = exchange(acc_far, ring, 3).transpose(1, 0, 2)
    near_acc = jnp.einsum("krs,rc->kcs", acc_near, near_owner, precision=lax.Precision.HIGHEST)
    back_acc = jnp.einsum("krs,rc->kcs", acc_back, sent_owner, precision=lax.Precision.HIGHEST)
    total_acc = local_force(positions, smooth, mass_eff, pressure) + near_acc + back_acc
    accel = jnp.where(occupied[None], total_acc, 0.0)
    return (density, accel)


def solution(mesh):
    in_specs = (
        P(("cells", "sub"), None, None),
        P(("cells", "sub"), None, None),
        P(("cells", "sub")),
        P(None, ("cells", "sub"), None),
        P(("cells", "sub"), None),
        P(("cells", "sub"), None),
        P(("cells", "sub"), None),
    )
    out_specs = (P(("cells", "sub"), None), P(None, ("cells", "sub"), None))
    return jax.shard_map(
        on_device, mesh=mesh, in_specs=in_specs, out_specs=out_specs, check_vma=False
    )
```

```python
import functools
import math

import jax
import jax.numpy as jnp
from jax import lax
from jax.experimental import pallas as pl
from jax.experimental.pallas import tpu as pltpu
from jax.sharding import PartitionSpec as P

KERNEL_NORM = 21.0 / (2.0 * math.pi)
LOGICAL = pl.DeviceIdType.LOGICAL
F32 = jnp.float32
BF16 = jnp.bfloat16


def rounded(value):
    return value.astype(BF16).astype(F32)


def three_pieces(value):
    first = rounded(value)
    rest = value - first
    second = rounded(rest)
    return first, second, rest - second


def dot_rows(left, right):
    return lax.dot_general(left, right, (((1,), (1,)), ((), ())), preferred_element_type=F32)


def dot_plain(left, right):
    return lax.dot_general(left, right, (((1,), (0,)), ((), ())), preferred_element_type=F32)


def pair_kernel(
    ring,
    peers,
    cells,
    slots,
    send_s,
    pair_s,
    counts_s,
    send_ref,
    pair_ref,
    pos_ref,
    mass_ref,
    smooth_ref,
    entropy_ref,
    density_ref,
    accel_ref,
    table,
    table_len,
    table_press,
    wide_len,
    aug,
    out_msg,
    in_msg,
    out_press,
    in_press,
    source_rows,
    dist,
    near_mats,
    far_mats,
    results,
    send_sem,
    recv_sem,
    send_sem2,
    recv_sem2,
    ready_sem,
):
    me = lax.axis_index(("cells", "sub"))
    local_next = cells - 1
    local_own = cells // 2
    local_count = local_next + local_own
    total_count = local_count + peers - 1
    stride = results.shape[0] // 8

    barrier = pltpu.get_barrier_semaphore()
    for step in range(1, ring):
        pl.semaphore_signal(barrier, inc=1, device_id=me ^ step, device_id_type=LOGICAL)
    for step in range(1, peers // ring):
        pl.semaphore_signal(
            barrier, inc=1, device_id=me ^ (ring * step), device_id_type=LOGICAL
        )

    row = lax.broadcasted_iota(jnp.int32, (8, slots), 0)
    upper = row < 4
    weight_row = (row == 3) | (row == 7)
    lane = lax.broadcasted_iota(jnp.int32, (1, slots), 1)

    for cell in range(cells):
        mass_row = jnp.where(lane < counts_s[cell], mass_ref[cell : cell + 1, :], 0.0)
        for half in (0, 4):
            for axis in range(3):
                table[cell, half + axis : half + axis + 1, :] = pos_ref[axis, cell : cell + 1, :]
            table[cell, half + 3 : half + 4, :] = mass_row
    table[cells] = jnp.zeros((8, slots), F32)
    table_len[0:cells, :] = smooth_ref[...]
    table_len[cells : cells + 8, :] = jnp.ones((8, slots), F32)
    table_press[cells : cells + 8, :] = jnp.zeros((8, slots), F32)
    results[...] = jnp.zeros(results.shape, F32)

    def fill_out(peer, carry):
        chosen = send_s[0, peer]
        first = jnp.where(chosen < 0, cells, chosen)
        second = pair_s[0, peer]
        out_msg[peer, 0:8, :] = jnp.where(upper, table[first], table[second])
        out_msg[peer, 8:9, :] = table_len[pl.ds(first, 1), :]
        out_msg[peer, 9:10, :] = table_len[pl.ds(second, 1), :]
        return carry

    lax.fori_loop(0, peers, fill_out, 0)

    pl.semaphore_wait(barrier, ring + peers // ring - 2)
    for step in range(1, ring):
        pl.semaphore_signal(ready_sem, inc=1, device_id=me ^ step, device_id_type=LOGICAL)
    pl.semaphore_wait(ready_sem, ring - 1)

    def send(step, carry):
        peer = me ^ step
        pltpu.make_async_remote_copy(
            src_ref=out_msg.at[peer],
            dst_ref=in_msg.at[me],
            send_sem=send_sem,
            recv_sem=recv_sem.at[me],
            device_id=peer,
            device_id_type=LOGICAL,
        ).start()
        return carry

    lax.fori_loop(1, peers, send, 0)

    def fill_local(index, first, second):
        in_msg[peers + index, 0:8, :] = jnp.where(upper, table[first], table[second])
        in_msg[peers + index, 8:9, :] = table_len[pl.ds(first, 1), :]
        in_msg[peers + index, 9:10, :] = table_len[pl.ds(second, 1), :]

    for cell in range(local_next):
        fill_local(cell, cell + 1, cell)
    for turn in range(local_own):
        fill_local(local_next + turn, 2 * turn, 2 * turn + 1)

    lens_t = jnp.transpose(table_len[0:cells, :])
    for cell in range(cells):
        wide = jnp.broadcast_to(lens_t[:, cell : cell + 1], (slots, slots))
        wide_len[cell] = wide
        own = table[cell]
        square = own * own
        total = pltpu.roll(square, 1, 0) + pltpu.roll(square, 2, 0) + pltpu.roll(square, 3, 0)
        p0, p1, p2 = three_pieces(jnp.where(weight_row, total, own))
        one = jnp.ones((8, slots), F32)
        q0 = jnp.where(weight_row, one, -2.0 * p0)
        q1 = jnp.where(weight_row, p0, -2.0 * p1)
        q2 = jnp.where(weight_row, p1, -2.0 * p2)
        q3 = q0
        q4 = jnp.where(weight_row, p2, -2.0 * p1)
        q5 = q0
        stack = jnp.concatenate(
            [
                jnp.where(upper, q0, q1),
                jnp.where(upper, q2, q3),
                jnp.where(upper, q4, q5),
                jnp.zeros((slots - 24, slots), F32),
            ],
            axis=0,
        )
        aug[cell] = jnp.transpose(stack)[:, 0:32].astype(BF16)

    def slot_of(turn):
        return jnp.where(turn < local_count, peers + turn, me ^ (turn - local_count + 1))

    def targets_of(turn):
        peer = jnp.where(turn < local_count, 0, me ^ (turn - local_count + 1))
        own = 2 * (turn - local_next)
        local_first = jnp.where(turn < local_next, turn, own)
        local_second = jnp.where(turn < local_next, turn + 1, own + 1)
        first = jnp.where(turn < local_count, local_first, pair_s[0, peer])
        second = jnp.where(turn < local_count, local_second, jnp.maximum(send_s[0, peer], 0))
        return first, second

    def stage_distance(turn):
        slot = slot_of(turn)
        first, second = targets_of(turn)
        data = in_msg[slot, 0:8, :]
        square = data * data
        total = pltpu.roll(square, 1, 0) + pltpu.roll(square, 2, 0) + pltpu.roll(square, 3, 0)
        p0, p1, p2 = three_pieces(jnp.where(weight_row, total, data))
        o0 = jnp.where(weight_row, 1.0, p0)
        o1 = jnp.where(weight_row, 1.0, p1)
        r0 = pltpu.roll(p0, 4, 0)
        r1 = pltpu.roll(p1, 4, 0)
        r2 = pltpu.roll(p2, 4, 0)
        s0 = pltpu.roll(o0, 4, 0)
        s1 = pltpu.roll(o1, 4, 0)
        zero = jnp.zeros((8, slots), F32)
        right_a = jnp.concatenate(
            [jnp.where(upper, p0, s0), jnp.where(upper, o0, r1), jnp.where(upper, o1, r2), zero],
            axis=0,
        ).astype(BF16)
        right_b = jnp.concatenate(
            [jnp.where(upper, r0, o0), jnp.where(upper, s0, p1), jnp.where(upper, s1, p2), zero],
            axis=0,
        ).astype(BF16)
        dist[0] = dot_plain(aug[first], right_a)
        dist[1] = dot_plain(aug[second], right_b)
        weight = jnp.where(upper, data[3:4, :], data[7:8, :])
        source_rows[slot] = weight * jnp.where(weight_row, 1.0, data)

    def split_store(ref, index, value):
        top = value.astype(BF16)
        ref[index + (slice(0, slots),)] = top
        ref[index + (slice(slots, 2 * slots),)] = (value - top.astype(F32)).astype(BF16)

    def stage_terms(turn):
        slot = slot_of(turn)
        pair_targets = targets_of(turn)
        for side in range(2):
            far_len = in_msg[slot, 8 + side : 9 + side, :]
            for block in range(0, slots, 16):
                rows = slice(block, block + 16)
                raw = jnp.maximum(dist[side, rows, :], 1e-30)
                radius = raw * lax.rsqrt(raw)
                len_i = wide_len[pair_targets[side], rows, :]
                t_i = jnp.maximum(len_i - radius, 0.0)
                cube = t_i * t_i * t_i
                value = cube * (t_i * (1.25 * len_i - t_i))
                t_j = jnp.maximum(far_len - radius, 0.0)
                cube_j = t_j * t_j * t_j
                base = 2 * side * slots + block
                split_store(near_mats, (slice(base, base + 16),), value)
                split_store(near_mats, (slice(base + slots, base + slots + 16),), cube)
                split_store(
                    far_mats, (slot, slice(side * slots + block, side * slots + block + 16)), cube_j
                )

    def stacked_pieces(value):
        p0, p1, p2 = three_pieces(value)
        stack = jnp.concatenate([p0, p1, p2, jnp.zeros((8, slots), F32)], axis=0).astype(BF16)
        return jnp.concatenate([stack, stack], axis=1)

    def sum_pieces(value):
        return value[0:8, :] + value[8:16, :] + value[16:24, :]

    def target_rows(turn):
        first, second = targets_of(turn)
        return jnp.where(upper, table[first], table[second])

    def moments(first_sums, second_sums, turn):
        sums = jnp.where(upper, first_sums, second_sums)
        weight = jnp.where(upper, first_sums[3:4, :], second_sums[7:8, :])
        return target_rows(turn) * weight - sums

    def stage_sums(turn):
        slot = slot_of(turn)
        found = sum_pieces(dot_rows(stacked_pieces(source_rows[slot]), near_mats[...]))
        dens = jnp.where(upper, found[:, 0:slots], found[:, 2 * slots : 3 * slots])
        slope = moments(found[:, slots : 2 * slots], found[:, 3 * slots : 4 * slots], turn)
        results[pl.ds(slot, 8, stride=stride), :] = jnp.where(weight_row, dens, slope)

    def wait_in(turn, ref, sem):
        slot = slot_of(turn)
        pltpu.make_async_copy(ref.at[slot], ref.at[slot], sem.at[slot]).wait()

    stage_distance(0)
    stage_terms(0)
    stage_distance(1)

    def local_turn(turn, carry):
        stage_sums(turn - 1)
        stage_terms(turn)
        stage_distance(turn + 1)
        return carry

    def far_turn(turn, carry):
        wait_in(turn + 1, in_msg, recv_sem)
        return local_turn(turn, carry)

    lax.fori_loop(1, local_count - 1, local_turn, 0)
    lax.fori_loop(local_count - 1, total_count - 1, far_turn, 0)
    stage_sums(total_count - 2)
    stage_terms(total_count - 1)
    stage_sums(total_count - 1)

    spare = stride - peers
    cell_ids = lax.broadcasted_iota(jnp.int32, (cells, peers), 0)
    extra = lax.broadcasted_iota(jnp.int32, (cells, spare), 1)
    extra_cell = lax.broadcasted_iota(jnp.int32, (cells, spare), 0)
    own_turn = 2 * (extra - local_next)
    is_next = extra < local_next
    is_own = (extra >= local_next) & (extra < local_count)
    extra_first = jnp.where(is_next, extra, jnp.where(is_own, own_turn, -1))
    extra_second = jnp.where(is_next, extra + 1, jnp.where(is_own, own_turn + 1, -1))

    def owner(keys, extra_keys):
        near = jnp.where(cell_ids == keys, 1.0, 0.0)
        local = jnp.where(extra_cell == extra_keys, 1.0, 0.0)
        return jnp.concatenate([near, local], axis=1).astype(BF16)

    owner_first = owner(pair_ref[...], extra_first)
    owner_second = owner(send_ref[...], extra_second)

    def summed(quantity):
        total = jnp.zeros((cells, slots), F32)
        for mat, at in ((owner_first, quantity), (owner_second, quantity + 4)):
            for piece in three_pieces(results[at * stride : (at + 1) * stride, :]):
                total = total + dot_plain(mat, piece.astype(BF16))
        return total

    lens = smooth_ref[...]
    len2 = lens * lens
    len4 = len2 * len2
    norm = KERNEL_NORM / (len4 * len4)
    cell_row = lax.broadcasted_iota(jnp.int32, (cells, slots), 0)
    limit = jnp.zeros((cells, slots), jnp.int32)
    for cell in range(cells):
        limit = jnp.where(cell_row == cell, counts_s[cell], limit)
    occupied = lax.broadcasted_iota(jnp.int32, (cells, slots), 1) < limit
    total = summed(3) * (4.0 * norm)
    safe = jnp.where(occupied, total, 1.0)
    pressure = entropy_ref[...] * jnp.exp(jnp.log(safe) * (-1.0 / 3.0))
    strength = jnp.where(occupied, pressure * (20.0 * norm), 0.0)
    density_ref[...] = jnp.where(occupied, total, 0.0)
    table_press[0:cells, :] = strength
    near_part = [summed(axis) * strength for axis in range(3)]

    def send_press(step, carry):
        peer = me ^ step
        chosen = send_s[0, peer]
        first = jnp.where(chosen < 0, cells, chosen)
        out_press[peer, 0:1, :] = table_press[pl.ds(first, 1), :]
        out_press[peer, 1:2, :] = table_press[pl.ds(pair_s[0, peer], 1), :]
        pltpu.make_async_remote_copy(
            src_ref=out_press.at[peer],
            dst_ref=in_press.at[me],
            send_sem=send_sem2,
            recv_sem=recv_sem2.at[me],
            device_id=peer,
            device_id_type=LOGICAL,
        ).start()
        return carry

    lax.fori_loop(1, peers, send_press, 0)

    def fill_press(index, first, second):
        in_press[peers + index, 0:1, :] = table_press[first : first + 1, :]
        in_press[peers + index, 1:2, :] = table_press[second : second + 1, :]

    for cell in range(local_next):
        fill_press(cell, cell + 1, cell)
    for turn in range(local_own):
        fill_press(local_next + turn, 2 * turn, 2 * turn + 1)

    def stage_force(turn):
        slot = slot_of(turn)
        press = jnp.where(upper, in_press[slot, 0:1, :], in_press[slot, 1:2, :])
        found = sum_pieces(dot_rows(stacked_pieces(source_rows[slot] * press), far_mats[slot]))
        slope = moments(found[:, 0:slots], found[:, slots : 2 * slots], turn)
        results[pl.ds(slot, 8, stride=stride), :] = slope

    def local_force(turn, carry):
        stage_force(turn)
        return carry

    def far_force(turn, carry):
        wait_in(turn, in_press, recv_sem2)
        stage_force(turn)
        return carry

    lax.fori_loop(0, local_count, local_force, 0)
    lax.fori_loop(local_count, total_count, far_force, 0)
    for axis in range(3):
        accel_ref[axis] = jnp.where(occupied, near_part[axis] + summed(axis), 0.0)

    def drain(ref, sem):
        moved = ref.at[pl.ds(0, peers - 1)]
        pltpu.make_async_copy(moved, moved, sem).wait()

    drain(out_msg, send_sem)
    drain(out_press, send_sem2)


def on_device(send_cells, pair_cell, counts, positions, mass, smooth, entropy):
    cells, slots = mass.shape
    peers = lax.axis_size(("cells", "sub"))
    ring = lax.axis_size("sub")
    chosen = send_cells.reshape(1, peers)
    partner = pair_cell.reshape(1, peers)
    stride = peers + 32
    vmem = pl.BlockSpec(memory_space=pltpu.VMEM)
    smem = pl.BlockSpec(memory_space=pltpu.SMEM)
    return pl.pallas_call(
        functools.partial(pair_kernel, ring, peers, cells, slots),
        out_shape=(
            jax.ShapeDtypeStruct((cells, slots), F32),
            jax.ShapeDtypeStruct((3, cells, slots), F32),
        ),
        in_specs=[smem, smem, smem] + [vmem] * 6,
        out_specs=(vmem, vmem),
        scratch_shapes=[
            pltpu.VMEM((cells + 1, 8, slots), F32),
            pltpu.VMEM((cells + 8, slots), F32),
            pltpu.VMEM((cells + 8, slots), F32),
            pltpu.VMEM((cells, slots, slots), F32),
            pltpu.VMEM((cells, slots, 32), BF16),
            pltpu.VMEM((peers, 10, slots), F32),
            pltpu.VMEM((stride, 10, slots), F32),
            pltpu.VMEM((peers, 2, slots), F32),
            pltpu.VMEM((stride, 2, slots), F32),
            pltpu.VMEM((stride, 8, slots), F32),
            pltpu.VMEM((2, slots, slots), F32),
            pltpu.VMEM((4 * slots, 2 * slots), BF16),
            pltpu.VMEM((stride, 2 * slots, 2 * slots), BF16),
            pltpu.VMEM((8 * stride, slots), F32),
            pltpu.SemaphoreType.DMA,
            pltpu.SemaphoreType.DMA((peers,)),
            pltpu.SemaphoreType.DMA,
            pltpu.SemaphoreType.DMA((peers,)),
            pltpu.SemaphoreType.REGULAR,
        ],
        compiler_params=pltpu.CompilerParams(
            collective_id=0, has_side_effects=True, vmem_limit_bytes=56 * 2**20
        ),
        name="cell_pairs",
    )(chosen, partner, counts, chosen, partner, positions, mass, smooth, entropy)


def solution(mesh):
    in_specs = (
        P(("cells", "sub"), None, None),
        P(("cells", "sub"), None, None),
        P(("cells", "sub")),
        P(None, ("cells", "sub"), None),
        P(("cells", "sub"), None),
        P(("cells", "sub"), None),
        P(("cells", "sub"), None),
    )
    out_specs = (P(("cells", "sub"), None), P(None, ("cells", "sub"), None))
    return jax.shard_map(
        on_device, mesh=mesh, in_specs=in_specs, out_specs=out_specs, check_vma=False
    )
```

```python
import functools
import math

import jax
import jax.numpy as jnp
from jax import lax
from jax.experimental import pallas as pl
from jax.experimental.pallas import tpu as pltpu
from jax.sharding import PartitionSpec as P

KERNEL_NORM = 21.0 / (2.0 * math.pi)
LOGICAL = pl.DeviceIdType.LOGICAL
F32 = jnp.float32
BF16 = jnp.bfloat16


def rounded(value):
    return value.astype(BF16).astype(F32)


def three_pieces(value):
    first = rounded(value)
    rest = value - first
    second = rounded(rest)
    return first, second, rest - second


def dot_rows(left, right):
    return lax.dot_general(left, right, (((1,), (1,)), ((), ())), preferred_element_type=F32)


def dot_plain(left, right):
    return lax.dot_general(left, right, (((1,), (0,)), ((), ())), preferred_element_type=F32)


def pair_kernel(
    ring,
    peers,
    cells,
    slots,
    send_s,
    pair_s,
    counts_s,
    send_ref,
    pair_ref,
    pos_ref,
    mass_ref,
    smooth_ref,
    entropy_ref,
    out_ref,
    table,
    table_len,
    table_press,
    wide_len,
    aug,
    aug_shift,
    out_msg,
    in_msg,
    out_press,
    in_press,
    source_rows,
    dist,
    near_mats,
    far_mats,
    results,
    send_sem,
    recv_sem,
    send_sem2,
    recv_sem2,
    ready_sem,
):
    me = lax.axis_index(("cells", "sub"))
    local_next = cells - 1
    local_own = cells // 2
    local_count = local_next + local_own
    total_count = local_count + peers - 1
    stride = results.shape[0] // 8

    barrier = pltpu.get_barrier_semaphore()
    for step in range(1, ring):
        pl.semaphore_signal(barrier, inc=1, device_id=me ^ step, device_id_type=LOGICAL)
    for step in range(1, peers // ring):
        pl.semaphore_signal(
            barrier, inc=1, device_id=me ^ (ring * step), device_id_type=LOGICAL
        )

    row = lax.broadcasted_iota(jnp.int32, (8, slots), 0)
    upper = row < 4
    weight_row = (row == 3) | (row == 7)
    lane = lax.broadcasted_iota(jnp.int32, (1, slots), 1)

    for cell in range(cells):
        mass_row = jnp.where(lane < counts_s[cell], mass_ref[cell : cell + 1, :], 0.0)
        for half in (0, 4):
            for axis in range(3):
                table[cell, half + axis : half + axis + 1, :] = pos_ref[axis, cell : cell + 1, :]
            table[cell, half + 3 : half + 4, :] = mass_row
    table[cells] = jnp.zeros((8, slots), F32)
    for cell in range(cells):
        table_len[cell] = jnp.broadcast_to(smooth_ref[cell : cell + 1, :], (8, slots))
    table_len[cells] = jnp.ones((8, slots), F32)
    table_press[cells] = jnp.zeros((8, slots), F32)
    results[...] = jnp.zeros(results.shape, F32)

    def fill_out(peer, carry):
        chosen = send_s[0, peer]
        first = jnp.where(chosen < 0, cells, chosen)
        second = pair_s[0, peer]
        out_msg[peer, 0:8, :] = jnp.where(upper, table[first], table[second])
        out_msg[peer, 8:10, :] = jnp.where(row < 1, table_len[first], table_len[second])[0:2, :]
        return carry

    lax.fori_loop(0, peers, fill_out, 0, unroll=4)

    pl.semaphore_wait(barrier, ring + peers // ring - 2)
    for step in range(1, ring):
        pl.semaphore_signal(ready_sem, inc=1, device_id=me ^ step, device_id_type=LOGICAL)
    pl.semaphore_wait(ready_sem, ring - 1)

    def send(step, carry):
        peer = me ^ step
        pltpu.make_async_remote_copy(
            src_ref=out_msg.at[peer],
            dst_ref=in_msg.at[me],
            send_sem=send_sem,
            recv_sem=recv_sem.at[me],
            device_id=peer,
            device_id_type=LOGICAL,
        ).start()
        return carry

    lax.fori_loop(1, peers, send, 0)

    def fill_local(index, first, second):
        in_msg[peers + index, 0:8, :] = jnp.where(upper, table[first], table[second])
        in_msg[peers + index, 8:9, :] = table_len[first, 0:1, :]
        in_msg[peers + index, 9:10, :] = table_len[second, 0:1, :]

    for cell in range(local_next):
        fill_local(cell, cell + 1, cell)
    for turn in range(local_own):
        fill_local(local_next + turn, 2 * turn, 2 * turn + 1)

    lens_t = jnp.transpose(smooth_ref[...])
    for cell in range(cells):
        wide = jnp.broadcast_to(lens_t[:, cell : cell + 1], (slots, slots))
        wide_len[cell] = wide
        own = table[cell]
        square = own * own
        total = pltpu.roll(square, 1, 0) + pltpu.roll(square, 2, 0) + pltpu.roll(square, 3, 0)
        p0, p1, p2 = three_pieces(jnp.where(weight_row, total, own))
        one = jnp.ones((8, slots), F32)
        q0 = jnp.where(weight_row, one, -2.0 * p0)
        q1 = jnp.where(weight_row, p0, -2.0 * p1)
        q2 = jnp.where(weight_row, p1, -2.0 * p2)
        q3 = q0
        q4 = jnp.where(weight_row, p2, -2.0 * p1)
        q5 = q0
        stack = jnp.concatenate(
            [
                jnp.where(upper, q0, q1),
                jnp.where(upper, q2, q3),
                jnp.where(upper, q4, q5),
                jnp.zeros((slots - 24, slots), F32),
            ],
            axis=0,
        )
        turned = jnp.transpose(stack)
        aug[cell] = turned.astype(BF16)
        aug_shift[cell] = pltpu.roll(turned, 32, 1).astype(BF16)

    def slot_of(turn):
        return jnp.where(turn < local_count, peers + turn, me ^ (turn - local_count + 1))

    def targets_of(turn):
        peer = jnp.where(turn < local_count, 0, me ^ (turn - local_count + 1))
        own = 2 * (turn - local_next)
        local_first = jnp.where(turn < local_next, turn, own)
        local_second = jnp.where(turn < local_next, turn + 1, own + 1)
        first = jnp.where(turn < local_count, local_first, pair_s[0, peer])
        second = jnp.where(turn < local_count, local_second, jnp.maximum(send_s[0, peer], 0))
        return first, second

    def stage_distance(turn, half):
        slot = slot_of(turn)
        first, second = targets_of(turn)
        data = in_msg[slot, 0:8, :]
        square = data * data
        total = pltpu.roll(square, 1, 0) + pltpu.roll(square, 2, 0) + pltpu.roll(square, 3, 0)
        p0, p1, p2 = three_pieces(jnp.where(weight_row, total, data))
        o0 = jnp.where(weight_row, 1.0, p0)
        o1 = jnp.where(weight_row, 1.0, p1)
        r0 = pltpu.roll(p0, 4, 0)
        r1 = pltpu.roll(p1, 4, 0)
        r2 = pltpu.roll(p2, 4, 0)
        s0 = pltpu.roll(o0, 4, 0)
        s1 = pltpu.roll(o1, 4, 0)
        zero = jnp.zeros((8, slots), F32)
        right_a = jnp.concatenate(
            [jnp.where(upper, p0, s0), jnp.where(upper, o0, r1), jnp.where(upper, o1, r2), zero],
            axis=0,
        ).astype(BF16)
        right_b = jnp.concatenate(
            [jnp.where(upper, r0, o0), jnp.where(upper, s0, p1), jnp.where(upper, s1, p2), zero],
            axis=0,
        ).astype(BF16)
        blank = jnp.zeros((32, slots), BF16)
        right = jnp.concatenate(
            [
                jnp.concatenate([right_a, blank], axis=1),
                jnp.concatenate([blank, right_b], axis=1),
            ],
            axis=0,
        )
        left = aug[first] + aug_shift[second]
        dist[half] = dot_plain(left[:, 0:64], right)
        weight = jnp.where(upper, data[3:4, :], data[7:8, :])
        source_rows[slot] = weight * jnp.where(weight_row, 1.0, data)

    def split_store(ref, index, value):
        top = value.astype(BF16)
        ref[index + (slice(0, slots),)] = top
        ref[index + (slice(slots, 2 * slots),)] = (value - top.astype(F32)).astype(BF16)

    def stage_terms(turn, half):
        slot = slot_of(turn)
        pair_targets = targets_of(turn)
        for side in range(2):
            far_len = in_msg[slot, 8 + side : 9 + side, :]
            for block in range(0, slots, 16):
                rows = slice(block, block + 16)
                raw = jnp.maximum(dist[half, rows, side * slots : (side + 1) * slots], 1e-30)
                radius = raw * lax.rsqrt(raw)
                len_i = wide_len[pair_targets[side], rows, :]
                t_i = jnp.maximum(len_i - radius, 0.0)
                cube = t_i * t_i * t_i
                value = cube * (t_i * (1.25 * len_i - t_i))
                t_j = jnp.maximum(far_len - radius, 0.0)
                cube_j = t_j * t_j * t_j
                base = 2 * side * slots + block
                split_store(near_mats, (half, slice(base, base + 16)), value)
                split_store(near_mats, (half, slice(base + slots, base + slots + 16)), cube)
                split_store(
                    far_mats, (slot, slice(side * slots + block, side * slots + block + 16)), cube_j
                )

    def stacked_pieces(value):
        p0, p1, p2 = three_pieces(value)
        stack = jnp.concatenate([p0, p1, p2, jnp.zeros((8, slots), F32)], axis=0).astype(BF16)
        return jnp.concatenate([stack, stack], axis=1)

    def sum_pieces(value):
        return value[0:8, :] + value[8:16, :] + value[16:24, :]

    def target_rows(turn):
        first, second = targets_of(turn)
        return jnp.where(upper, table[first], table[second])

    def moments(first_sums, second_sums, turn):
        sums = jnp.where(upper, first_sums, second_sums)
        weight = jnp.where(upper, first_sums[3:4, :], second_sums[7:8, :])
        return target_rows(turn) * weight - sums

    def stage_sums(turn, half):
        slot = slot_of(turn)
        found = sum_pieces(dot_rows(stacked_pieces(source_rows[slot]), near_mats[half]))
        dens = jnp.where(upper, found[:, 0:slots], found[:, 2 * slots : 3 * slots])
        slope = moments(found[:, slots : 2 * slots], found[:, 3 * slots : 4 * slots], turn)
        results[pl.ds(slot, 8, stride=stride), :] = jnp.where(weight_row, dens, slope)

    def wait_in(turn, ref, sem):
        slot = slot_of(turn)
        pltpu.make_async_copy(ref.at[slot], ref.at[slot], sem.at[slot]).wait()

    def local_turn(turn, carry):
        stage_sums(2 * turn - 1, 1)
        stage_terms(2 * turn, 0)
        stage_distance(2 * turn + 2, 0)
        stage_sums(2 * turn, 0)
        stage_terms(2 * turn + 1, 1)
        stage_distance(2 * turn + 3, 1)
        return carry

    def far_turn(turn, carry):
        wait_in(2 * turn + 2, in_msg, recv_sem)
        wait_in(2 * turn + 3, in_msg, recv_sem)
        return local_turn(turn, carry)

    turns = total_count // 2
    mixed = local_count // 2
    stage_distance(0, 0)
    stage_distance(1, 1)
    stage_terms(0, 0)
    stage_distance(2, 0)
    stage_sums(0, 0)
    stage_terms(1, 1)
    stage_distance(3, 1)
    lax.fori_loop(1, mixed - 1, local_turn, 0)
    wait_in(2 * mixed + 1, in_msg, recv_sem)
    local_turn(mixed - 1, 0)
    lax.fori_loop(mixed, turns - 1, far_turn, 0)
    stage_sums(total_count - 3, 1)
    stage_terms(total_count - 2, 0)
    stage_sums(total_count - 2, 0)
    stage_terms(total_count - 1, 1)
    stage_sums(total_count - 1, 1)

    spare = stride - peers
    cell_ids = lax.broadcasted_iota(jnp.int32, (cells, peers), 0)
    extra = lax.broadcasted_iota(jnp.int32, (cells, spare), 1)
    extra_cell = lax.broadcasted_iota(jnp.int32, (cells, spare), 0)
    own_turn = 2 * (extra - local_next)
    is_next = extra < local_next
    is_own = (extra >= local_next) & (extra < local_count)
    extra_first = jnp.where(is_next, extra, jnp.where(is_own, own_turn, -1))
    extra_second = jnp.where(is_next, extra + 1, jnp.where(is_own, own_turn + 1, -1))

    def owner(keys, extra_keys):
        near = jnp.where(cell_ids == keys, 1.0, 0.0)
        local = jnp.where(extra_cell == extra_keys, 1.0, 0.0)
        return jnp.concatenate([near, local], axis=1).astype(BF16)

    owner_first = owner(pair_ref[...], extra_first)
    owner_second = owner(send_ref[...], extra_second)

    def summed(quantity):
        total = jnp.zeros((cells, slots), F32)
        for mat, at in ((owner_first, quantity), (owner_second, quantity + 4)):
            for piece in three_pieces(results[at * stride : (at + 1) * stride, :]):
                total = total + dot_plain(mat, piece.astype(BF16))
        return total

    lens = smooth_ref[...]
    len2 = lens * lens
    len4 = len2 * len2
    norm = KERNEL_NORM / (len4 * len4)
    cell_row = lax.broadcasted_iota(jnp.int32, (cells, slots), 0)
    limit = jnp.zeros((cells, slots), jnp.int32)
    for cell in range(cells):
        limit = jnp.where(cell_row == cell, counts_s[cell], limit)
    occupied = lax.broadcasted_iota(jnp.int32, (cells, slots), 1) < limit
    total = summed(3) * (4.0 * norm)
    safe = jnp.where(occupied, total, 1.0)
    pressure = entropy_ref[...] * jnp.exp(jnp.log(safe) * (-1.0 / 3.0))
    strength = jnp.where(occupied, pressure * (20.0 * norm), 0.0)
    out_ref[0] = jnp.where(occupied, total, 0.0)
    for cell in range(cells):
        table_press[cell] = jnp.broadcast_to(strength[cell : cell + 1, :], (8, slots))
    near_part = [summed(axis) * strength for axis in range(3)]

    def send_press(step, carry):
        peer = me ^ step
        chosen = send_s[0, peer]
        first = jnp.where(chosen < 0, cells, chosen)
        second = pair_s[0, peer]
        out_press[peer] = jnp.where(row < 1, table_press[first], table_press[second])[0:2, :]
        pltpu.make_async_remote_copy(
            src_ref=out_press.at[peer],
            dst_ref=in_press.at[me],
            send_sem=send_sem2,
            recv_sem=recv_sem2.at[me],
            device_id=peer,
            device_id_type=LOGICAL,
        ).start()
        return carry

    lax.fori_loop(1, peers, send_press, 0)

    def fill_press(index, first, second):
        in_press[peers + index, 0:1, :] = table_press[first, 0:1, :]
        in_press[peers + index, 1:2, :] = table_press[second, 0:1, :]

    for cell in range(local_next):
        fill_press(cell, cell + 1, cell)
    for turn in range(local_own):
        fill_press(local_next + turn, 2 * turn, 2 * turn + 1)

    def stage_force(turn):
        slot = slot_of(turn)
        press = jnp.where(upper, in_press[slot, 0:1, :], in_press[slot, 1:2, :])
        found = sum_pieces(dot_rows(stacked_pieces(source_rows[slot] * press), far_mats[slot]))
        slope = moments(found[:, 0:slots], found[:, slots : 2 * slots], turn)
        results[pl.ds(slot, 8, stride=stride), :] = slope

    group = 4

    def far_force(turn, carry):
        for step in range(group):
            wait_in(local_count + group * turn + step, in_press, recv_sem2)
        for step in range(group):
            stage_force(local_count + group * turn + step)
        return carry

    far_groups = (peers - 1) // group
    for turn in range(local_count):
        stage_force(turn)
    lax.fori_loop(0, far_groups, far_force, 0)
    for turn in range(local_count + group * far_groups, total_count):
        wait_in(turn, in_press, recv_sem2)
    for turn in range(local_count + group * far_groups, total_count):
        stage_force(turn)
    for axis in range(3):
        out_ref[1 + axis] = jnp.where(occupied, near_part[axis] + summed(axis), 0.0)

    def drain(ref, sem):
        moved = ref.at[pl.ds(0, peers - 1)]
        pltpu.make_async_copy(moved, moved, sem).wait()

    drain(out_msg, send_sem)
    drain(out_press, send_sem2)


def split_kernel(found_ref, density_ref, accel_ref):
    density_ref[...] = found_ref[0]
    accel_ref[...] = found_ref[1:4]


def on_device(send_cells, pair_cell, counts, positions, mass, smooth, entropy):
    cells, slots = mass.shape
    peers = lax.axis_size(("cells", "sub"))
    ring = lax.axis_size("sub")
    chosen = send_cells.reshape(1, peers)
    partner = pair_cell.reshape(1, peers)
    stride = peers + 32
    vmem = pl.BlockSpec(memory_space=pltpu.VMEM)
    smem = pl.BlockSpec(memory_space=pltpu.SMEM)
    found = pl.pallas_call(
        functools.partial(pair_kernel, ring, peers, cells, slots),
        out_shape=jax.ShapeDtypeStruct((4, cells, slots), F32),
        in_specs=[smem, smem, smem] + [vmem] * 6,
        out_specs=vmem,
        scratch_shapes=[
            pltpu.VMEM((cells + 1, 8, slots), F32),
            pltpu.VMEM((cells + 1, 8, slots), F32),
            pltpu.VMEM((cells + 1, 8, slots), F32),
            pltpu.VMEM((cells, slots, slots), F32),
            pltpu.VMEM((cells, slots, slots), BF16),
            pltpu.VMEM((cells, slots, slots), BF16),
            pltpu.VMEM((peers, 10, slots), F32),
            pltpu.VMEM((stride, 10, slots), F32),
            pltpu.VMEM((peers, 2, slots), F32),
            pltpu.VMEM((stride, 2, slots), F32),
            pltpu.VMEM((stride, 8, slots), F32),
            pltpu.VMEM((2, slots, 2 * slots), F32),
            pltpu.VMEM((2, 4 * slots, 2 * slots), BF16),
            pltpu.VMEM((stride, 2 * slots, 2 * slots), BF16),
            pltpu.VMEM((8 * stride, slots), F32),
            pltpu.SemaphoreType.DMA,
            pltpu.SemaphoreType.DMA((peers,)),
            pltpu.SemaphoreType.DMA,
            pltpu.SemaphoreType.DMA((peers,)),
            pltpu.SemaphoreType.REGULAR,
        ],
        compiler_params=pltpu.CompilerParams(
            collective_id=0, has_side_effects=True, vmem_limit_bytes=56 * 2**20
        ),
        name="cell_pairs",
    )(chosen, partner, counts, chosen, partner, positions, mass, smooth, entropy)
    return pl.pallas_call(
        split_kernel,
        out_shape=(
            jax.ShapeDtypeStruct((cells, slots), F32),
            jax.ShapeDtypeStruct((3, cells, slots), F32),
        ),
        in_specs=[vmem],
        out_specs=(vmem, vmem),
        name="split_outputs",
    )(found)


def solution(mesh):
    in_specs = (
        P(("cells", "sub"), None, None),
        P(("cells", "sub"), None, None),
        P(("cells", "sub")),
        P(None, ("cells", "sub"), None),
        P(("cells", "sub"), None),
        P(("cells", "sub"), None),
        P(("cells", "sub"), None),
    )
    out_specs = (P(("cells", "sub"), None), P(None, ("cells", "sub"), None))
    return jax.shard_map(
        on_device, mesh=mesh, in_specs=in_specs, out_specs=out_specs, check_vma=False
    )
```

```python
import functools
import math

import jax
import jax.numpy as jnp
from jax import lax
from jax.experimental import pallas as pl
from jax.experimental.pallas import tpu as pltpu
from jax.sharding import PartitionSpec as P

KERNEL_NORM = 21.0 / (2.0 * math.pi)
CENTRE = 0.75
LOGICAL = pl.DeviceIdType.LOGICAL
F32 = jnp.float32
BF16 = jnp.bfloat16


def rounded(value):
    return value.astype(BF16).astype(F32)


def three_pieces(value):
    first = rounded(value)
    rest = value - first
    second = rounded(rest)
    return first, second, rest - second


def dot_rows(left, right):
    return lax.dot_general(left, right, (((1,), (1,)), ((), ())), preferred_element_type=F32)


def dot_plain(left, right):
    return lax.dot_general(left, right, (((1,), (0,)), ((), ())), preferred_element_type=F32)


def pair_kernel(
    ring,
    peers,
    cells,
    slots,
    send_s,
    pair_s,
    counts_s,
    send_ref,
    pair_ref,
    pos_ref,
    mass_ref,
    smooth_ref,
    entropy_ref,
    out_ref,
    table,
    table_len,
    table_press,
    table_gap,
    columns,
    fourths,
    aug,
    out_msg,
    in_msg,
    out_press,
    in_press,
    source_rows,
    source_stack,
    dist,
    near_mats,
    far_mats,
    results,
    send_sem,
    recv_sem,
    send_sem2,
    recv_sem2,
    ready_sem,
):
    me = lax.axis_index(("cells", "sub"))
    local_next = cells - 1
    local_own = cells // 2
    local_count = local_next + local_own
    total_count = local_count + peers - 1
    stride = results.shape[0] // 8

    barrier = pltpu.get_barrier_semaphore()
    for step in range(1, ring):
        pl.semaphore_signal(barrier, inc=1, device_id=me ^ step, device_id_type=LOGICAL)
    for step in range(1, peers // ring):
        pl.semaphore_signal(
            barrier, inc=1, device_id=me ^ (ring * step), device_id_type=LOGICAL
        )

    row = lax.broadcasted_iota(jnp.int32, (8, slots), 0)
    upper = row < 4
    weight_row = (row == 3) | (row == 7)
    lane = lax.broadcasted_iota(jnp.int32, (1, slots), 1)

    for cell in range(cells):
        mass_row = jnp.where(lane < counts_s[cell], mass_ref[cell : cell + 1, :], 0.0)
        for half in (0, 4):
            for axis in range(3):
                row_at = half + axis
                table[cell, row_at : row_at + 1, :] = pos_ref[axis, cell : cell + 1, :] - CENTRE
            table[cell, half + 3 : half + 4, :] = mass_row
    table[cells] = jnp.zeros((8, slots), F32)
    for cell in range(cells):
        table_len[cell] = jnp.broadcast_to(smooth_ref[cell : cell + 1, :], (8, slots))
    table_len[cells] = jnp.ones((8, slots), F32)
    table_press[cells] = jnp.zeros((8, slots), F32)
    results[...] = jnp.zeros(results.shape, F32)

    def fill_out(step, carry):
        peer = me ^ step
        chosen = send_s[0, peer]
        first = jnp.where(chosen < 0, cells, chosen)
        second = pair_s[0, peer]
        out_msg[step, 0:8, :] = jnp.where(upper, table[first], table[second])
        out_msg[step, 8:10, :] = jnp.where(row < 1, table_len[first], table_len[second])[0:2, :]
        return carry

    lax.fori_loop(0, peers, fill_out, 0, unroll=4)

    def fill_local(index, first, second):
        in_msg[peers + index, 0:8, :] = jnp.where(upper, table[first], table[second])
        in_msg[peers + index, 8:9, :] = table_len[first, 0:1, :]
        in_msg[peers + index, 9:10, :] = table_len[second, 0:1, :]

    for cell in range(local_next):
        fill_local(cell, cell + 1, cell)
    for turn in range(local_own):
        fill_local(local_next + turn, 2 * turn, 2 * turn + 1)

    blank = jnp.zeros((8, slots), F32)
    for cell in range(cells):
        own = table[cell]
        square = own * own
        total = pltpu.roll(square, 1, 0) + pltpu.roll(square, 2, 0) + pltpu.roll(square, 3, 0)
        own_len = table_len[cell]
        table_gap[cell] = own_len * own_len - total
        p0, p1, p2 = three_pieces(jnp.where(weight_row, total, own))
        one = jnp.ones((8, slots), F32)
        q0 = jnp.where(weight_row, one, -2.0 * p0)
        q1 = jnp.where(weight_row, p0, -2.0 * p1)
        q2 = jnp.where(weight_row, p1, -2.0 * p2)
        q4 = jnp.where(weight_row, p2, -2.0 * p1)
        parts = [jnp.where(upper, q0, q1), jnp.where(upper, q2, q0), jnp.where(upper, q4, q0)]
        aug[cell, 0] = jnp.concatenate(parts + [blank] * 5, axis=0).astype(BF16)
        aug[cell, 1] = jnp.concatenate([blank] * 3 + parts + [blank] * 2, axis=0).astype(BF16)

    pl.semaphore_wait(barrier, ring + peers // ring - 2)
    for step in range(1, ring):
        pl.semaphore_signal(ready_sem, inc=1, device_id=me ^ step, device_id_type=LOGICAL)

    def copy_out(step, source, target, sent, received):
        pltpu.make_async_remote_copy(
            src_ref=source.at[step],
            dst_ref=target.at[step],
            send_sem=sent,
            recv_sem=received.at[(step + 2) // 4],
            device_id=me ^ step,
            device_id_type=LOGICAL,
        ).start()

    def wait_in(group, count, ref, sem):
        got = ref.at[pl.ds(0, count)]
        pltpu.make_async_copy(got, got, sem.at[group]).wait()

    def slot_of(turn):
        return jnp.where(turn < local_count, peers + turn, turn - local_count + 1)

    def targets_of(turn):
        peer = jnp.where(turn < local_count, 0, me ^ (turn - local_count + 1))
        own = 2 * (turn - local_next)
        local_first = jnp.where(turn < local_next, turn, own)
        local_second = jnp.where(turn < local_next, turn + 1, own + 1)
        first = jnp.where(turn < local_count, local_first, pair_s[0, peer])
        second = jnp.where(turn < local_count, local_second, jnp.maximum(send_s[0, peer], 0))
        return first, second

    def stage_distance(turn, half):
        slot = slot_of(turn)
        first, second = targets_of(turn)
        data = in_msg[slot, 0:8, :]
        square = data * data
        total = pltpu.roll(square, 1, 0) + pltpu.roll(square, 2, 0) + pltpu.roll(square, 3, 0)
        p0, p1, p2 = three_pieces(jnp.where(weight_row, total, data))
        o0 = jnp.where(weight_row, 1.0, p0)
        o1 = jnp.where(weight_row, 1.0, p1)
        r0 = pltpu.roll(p0, 4, 0)
        r1 = pltpu.roll(p1, 4, 0)
        r2 = pltpu.roll(p2, 4, 0)
        s0 = pltpu.roll(o0, 4, 0)
        s1 = pltpu.roll(o1, 4, 0)
        far_len = in_msg[slot, 8:10, :]
        masses = jnp.where(row < 3, data[3:4, :], data[7:8, :])
        stack = jnp.concatenate(
            [
                jnp.where(upper, p0, s0),
                jnp.where(upper, o0, r1),
                jnp.where(upper, o1, r2),
                jnp.where(upper, r0, o0),
                jnp.where(upper, s0, p1),
                jnp.where(upper, s1, p2),
                jnp.where(row < 1, far_len[0:1, :], jnp.where(row < 2, far_len[1:2, :], masses)),
                jnp.zeros((8, slots), F32),
            ],
            axis=0,
        )
        turned = jnp.transpose(stack)
        right = jnp.concatenate([aug[first, 0], aug[second, 1]], axis=1)
        dist[half] = dot_plain(turned.astype(BF16), right)
        columns[half] = turned
        weight = jnp.where(upper, data[3:4, :], data[7:8, :])
        rows = weight * jnp.where(weight_row, 1.0, data)
        source_rows[slot] = rows
        m0, m1, m2 = three_pieces(rows)
        v0, v1, v2 = three_pieces(weight * total)
        v1 = pltpu.roll(v1, 7, 0)
        v2 = pltpu.roll(v2, 6, 0)
        squares = jnp.where(weight_row, v0, jnp.where((row == 2) | (row == 6), v1, v2))
        source_stack[half] = jnp.concatenate([m0, m1, m2, squares], axis=0).astype(BF16)

    def split_store(ref, index, block, lanes, value):
        top = value.astype(BF16)
        lanes = slice(lanes, lanes + slots)
        ref[index + (slice(block, block + 16), lanes)] = top
        rest = (value - top.astype(F32)).astype(BF16)
        ref[index + (slice(slots + block, slots + block + 16), lanes)] = rest

    def stage_terms(turn, half):
        slot = slot_of(turn)
        pair_targets = targets_of(turn)
        for side in range(2):
            len_i = table_len[pair_targets[side], 0:1, :]
            fourth = jnp.zeros((8, slots), F32)
            for block in range(0, slots, 16):
                rows = slice(block, block + 16)
                raw = jnp.maximum(dist[half, rows, side * slots : (side + 1) * slots], 1e-30)
                radius = raw * lax.rsqrt(raw)
                t_i = jnp.maximum(len_i - radius, 0.0)
                cube = t_i * t_i * t_i
                t_j = jnp.maximum(columns[half, rows, 48 + side : 49 + side] - radius, 0.0)
                split_store(near_mats, (half,), block, side * slots, cube)
                split_store(far_mats, (slot,), block, side * slots, t_j * t_j * t_j)
                term = cube * t_i * columns[half, rows, 50 + side : 51 + side]
                fourth = fourth + term[0:8, :] + term[8:16, :]
            for shift in (4, 2, 1):
                fourth = fourth + pltpu.roll(fourth, shift, 0)
            fourths[half, side] = fourth

    def stacked_pieces(value):
        p0, p1, p2 = three_pieces(value)
        stack = jnp.concatenate([p0, p1, p2, jnp.zeros((8, slots), F32)], axis=0).astype(BF16)
        return jnp.concatenate([stack, stack], axis=1)

    def sum_pieces(value):
        return value[0:8, :] + value[8:16, :] + value[16:24, :]

    def target_rows(turn):
        first, second = targets_of(turn)
        return jnp.where(upper, table[first], table[second])

    def moments(first_sums, second_sums, turn):
        sums = jnp.where(upper, first_sums, second_sums)
        weight = jnp.where(upper, first_sums[3:4, :], second_sums[7:8, :])
        return target_rows(turn) * weight - sums

    def stage_sums(turn, half):
        slot = slot_of(turn)
        first, second = targets_of(turn)
        stack = source_stack[half]
        left = jnp.concatenate([stack, stack], axis=1)
        found = dot_plain(left, near_mats[half])

        def piece(at):
            return jnp.where(upper, found[at : at + 8, 0:slots], found[at : at + 8, slots:])

        cubes = piece(0) + piece(8) + piece(16)
        square = piece(24)
        fourth = jnp.where(upper, fourths[half, 0], fourths[half, 1])
        square = square + pltpu.roll(square, 1, 0) + pltpu.roll(square, 2, 0)
        place = jnp.where(upper, table[first], table[second])
        gap = jnp.where(upper, table_gap[first], table_gap[second])
        length = jnp.where(upper, table_len[first], table_len[second])
        weight = jnp.where(upper, cubes[3:4, :], cubes[7:8, :])
        cross = place * cubes
        cross = pltpu.roll(cross, 1, 0) + pltpu.roll(cross, 2, 0) + pltpu.roll(cross, 3, 0)
        dens = gap * weight + 2.0 * cross - square - 0.75 * length * fourth
        slope = place * weight - cubes
        results[pl.ds(slot, 8, stride=stride), :] = jnp.where(weight_row, dens, slope)

    def sums(turn, bank):
        stage_sums(2 * turn, 2 * bank)
        stage_sums(2 * turn + 1, 2 * bank + 1)

    def terms(turn, bank):
        stage_terms(2 * turn, 2 * bank)
        stage_terms(2 * turn + 1, 2 * bank + 1)

    def distances(turn, bank):
        stage_distance(2 * turn, 2 * bank)
        stage_distance(2 * turn + 1, 2 * bank + 1)

    def full_turn(turn, bank):
        sums(turn - 1, 1 - bank)
        terms(turn, bank)
        distances(turn + 1, 1 - bank)

    turns = total_count // 2
    mixed = local_count // 2
    local_steps = (mixed - 2) // 2
    early_steps = local_steps - 2

    def local_step(step, carry):
        full_turn(2 * step + 1, 1)
        full_turn(2 * step + 2, 0)
        return carry

    def far_step(step, carry):
        turn = 2 * step + mixed
        wait_in(step + 1, 4, in_msg, recv_sem)
        full_turn(turn, mixed % 2)
        full_turn(turn + 1, (mixed + 1) % 2)
        return carry

    distances(0, 0)
    terms(0, 0)
    distances(1, 1)
    lax.fori_loop(0, early_steps, local_step, 0)
    pl.semaphore_wait(ready_sem, ring - 1)

    def send(step, carry):
        copy_out(step, out_msg, in_msg, send_sem, recv_sem)
        return carry

    lax.fori_loop(1, peers, send, 0)
    lax.fori_loop(early_steps, local_steps, local_step, 0)
    for turn in range(2 * local_steps + 1, mixed):
        if turn == mixed - 1:
            wait_in(0, 1, in_msg, recv_sem)
        full_turn(turn, turn % 2)
    steps = (turns - 1 - mixed) // 2
    lax.fori_loop(0, steps, far_step, 0)
    rest = (peers - 2) % 4
    for turn in range(mixed + 2 * steps, turns - 1):
        wait_in(steps + 1, rest, in_msg, recv_sem)
        full_turn(turn, turn % 2)
    sums(turns - 2, turns % 2)
    terms(turns - 1, (turns - 1) % 2)
    sums(turns - 1, (turns - 1) % 2)

    spare = stride - peers
    cell_ids = lax.broadcasted_iota(jnp.int32, (cells, peers), 0)
    extra = lax.broadcasted_iota(jnp.int32, (cells, spare), 1)
    extra_cell = lax.broadcasted_iota(jnp.int32, (cells, spare), 0)
    own_turn = 2 * (extra - local_next)
    is_next = extra < local_next
    is_own = (extra >= local_next) & (extra < local_count)
    extra_first = jnp.where(is_next, extra, jnp.where(is_own, own_turn, -1))
    extra_second = jnp.where(is_next, extra + 1, jnp.where(is_own, own_turn + 1, -1))

    from_peer = lax.broadcasted_iota(jnp.int32, (peers, peers), 0)
    at_step = lax.broadcasted_iota(jnp.int32, (peers, peers), 1)
    order = jnp.where(from_peer == at_step ^ me, 1.0, 0.0).astype(BF16)

    def by_step(keys):
        wide_keys = jnp.broadcast_to(keys.astype(F32), (16, peers)).astype(BF16)
        return dot_plain(wide_keys, order)[0:1, :].astype(jnp.int32)

    def owner(keys, extra_keys):
        near = jnp.where(cell_ids == keys, 1.0, 0.0)
        local = jnp.where(extra_cell == extra_keys, 1.0, 0.0)
        return jnp.concatenate([near, local], axis=1).astype(BF16)

    owner_first = owner(by_step(pair_ref[...]), extra_first)
    owner_second = owner(by_step(send_ref[...]), extra_second)

    def summed(quantity):
        total = jnp.zeros((cells, slots), F32)
        for mat, at in ((owner_first, quantity), (owner_second, quantity + 4)):
            for piece in three_pieces(results[at * stride : (at + 1) * stride, :]):
                total = total + dot_plain(mat, piece.astype(BF16))
        return total

    lens = smooth_ref[...]
    len2 = lens * lens
    len4 = len2 * len2
    norm = KERNEL_NORM / (len4 * len4)
    cell_row = lax.broadcasted_iota(jnp.int32, (cells, slots), 0)
    limit = jnp.zeros((cells, slots), jnp.int32)
    for cell in range(cells):
        limit = jnp.where(cell_row == cell, counts_s[cell], limit)
    occupied = lax.broadcasted_iota(jnp.int32, (cells, slots), 1) < limit
    total = summed(3) * (4.0 * norm)
    safe = jnp.where(occupied, total, 1.0)
    pressure = entropy_ref[...] * jnp.exp(jnp.log(safe) * (-1.0 / 3.0))
    strength = jnp.where(occupied, pressure * (20.0 * norm), 0.0)
    out_ref[0] = jnp.where(occupied, total, 0.0)
    for cell in range(cells):
        table_press[cell] = jnp.broadcast_to(strength[cell : cell + 1, :], (8, slots))
    near_part = [summed(axis) * strength for axis in range(3)]

    def send_press(step, carry):
        peer = me ^ step
        chosen = send_s[0, peer]
        first = jnp.where(chosen < 0, cells, chosen)
        second = pair_s[0, peer]
        out_press[step] = jnp.where(row < 1, table_press[first], table_press[second])[0:2, :]
        copy_out(step, out_press, in_press, send_sem2, recv_sem2)
        return carry

    lax.fori_loop(1, peers, send_press, 0, unroll=2)

    def fill_press(index, first, second):
        in_press[peers + index, 0:1, :] = table_press[first, 0:1, :]
        in_press[peers + index, 1:2, :] = table_press[second, 0:1, :]

    for cell in range(local_next):
        fill_press(cell, cell + 1, cell)
    for turn in range(local_own):
        fill_press(local_next + turn, 2 * turn, 2 * turn + 1)

    def stage_force(turn):
        slot = slot_of(turn)
        press = jnp.where(upper, in_press[slot, 0:1, :], in_press[slot, 1:2, :])
        found = sum_pieces(dot_plain(stacked_pieces(source_rows[slot] * press), far_mats[slot]))
        slope = moments(found[:, 0:slots], found[:, slots : 2 * slots], turn)
        results[pl.ds(slot, 8, stride=stride), :] = slope

    for turn in range(local_count):
        stage_force(turn)

    def far_force(step, carry):
        wait_in(step + 1, 4, in_press, recv_sem2)
        for at in range(4):
            stage_force(local_count + 1 + 4 * step + at)
        return carry

    wait_in(0, 1, in_press, recv_sem2)
    stage_force(local_count)
    steps = (peers - 2) // 4
    lax.fori_loop(0, steps, far_force, 0)
    wait_in(steps + 1, rest, in_press, recv_sem2)
    for at in range(rest):
        stage_force(local_count + 1 + 4 * steps + at)
    for axis in range(3):
        out_ref[1 + axis] = jnp.where(occupied, near_part[axis] + summed(axis), 0.0)

    def drain(ref, sem):
        moved = ref.at[pl.ds(0, peers - 1)]
        pltpu.make_async_copy(moved, moved, sem).wait()

    drain(out_msg, send_sem)
    drain(out_press, send_sem2)


def split_kernel(found_ref, density_ref, accel_ref):
    density_ref[...] = found_ref[0]
    accel_ref[...] = found_ref[1:4]


def on_device(send_cells, pair_cell, counts, positions, mass, smooth, entropy):
    cells, slots = mass.shape
    peers = lax.axis_size(("cells", "sub"))
    ring = lax.axis_size("sub")
    chosen = send_cells.reshape(1, peers)
    partner = pair_cell.reshape(1, peers)
    stride = peers + 32
    vmem = pl.BlockSpec(memory_space=pltpu.VMEM)
    smem = pl.BlockSpec(memory_space=pltpu.SMEM)
    found = pl.pallas_call(
        functools.partial(pair_kernel, ring, peers, cells, slots),
        out_shape=jax.ShapeDtypeStruct((4, cells, slots), F32),
        in_specs=[smem, smem, smem] + [vmem] * 6,
        out_specs=vmem,
        scratch_shapes=[
            pltpu.VMEM((cells + 1, 8, slots), F32),
            pltpu.VMEM((cells + 1, 8, slots), F32),
            pltpu.VMEM((cells + 1, 8, slots), F32),
            pltpu.VMEM((cells, 8, slots), F32),
            pltpu.VMEM((4, slots, 64), F32),
            pltpu.VMEM((4, 2, 8, slots), F32),
            pltpu.VMEM((cells, 2, 64, slots), BF16),
            pltpu.VMEM((peers, 10, slots), F32),
            pltpu.VMEM((stride, 10, slots), F32),
            pltpu.VMEM((peers, 2, slots), F32),
            pltpu.VMEM((stride, 2, slots), F32),
            pltpu.VMEM((stride, 8, slots), F32),
            pltpu.VMEM((4, 32, slots), BF16),
            pltpu.VMEM((4, slots, 2 * slots), F32),
            pltpu.VMEM((4, 2 * slots, 2 * slots), BF16),
            pltpu.VMEM((stride, 2 * slots, 2 * slots), BF16),
            pltpu.VMEM((8 * stride, slots), F32),
            pltpu.SemaphoreType.DMA,
            pltpu.SemaphoreType.DMA(((peers + 1) // 4 + 1,)),
            pltpu.SemaphoreType.DMA,
            pltpu.SemaphoreType.DMA(((peers + 1) // 4 + 1,)),
            pltpu.SemaphoreType.REGULAR,
        ],
        compiler_params=pltpu.CompilerParams(
            collective_id=0, has_side_effects=True, vmem_limit_bytes=56 * 2**20
        ),
        name="cell_pairs",
    )(chosen, partner, counts, chosen, partner, positions, mass, smooth, entropy)
    return pl.pallas_call(
        split_kernel,
        out_shape=(
            jax.ShapeDtypeStruct((cells, slots), F32),
            jax.ShapeDtypeStruct((3, cells, slots), F32),
        ),
        in_specs=[vmem],
        out_specs=(vmem, vmem),
        name="split_outputs",
    )(found)


def solution(mesh):
    in_specs = (
        P(("cells", "sub"), None, None),
        P(("cells", "sub"), None, None),
        P(("cells", "sub")),
        P(None, ("cells", "sub"), None),
        P(("cells", "sub"), None),
        P(("cells", "sub"), None),
        P(("cells", "sub"), None),
    )
    out_specs = (P(("cells", "sub"), None), P(None, ("cells", "sub"), None))
    return jax.shard_map(
        on_device, mesh=mesh, in_specs=in_specs, out_specs=out_specs, check_vma=False
    )
```

```python
import functools
import math

import jax
import jax.numpy as jnp
from jax import lax
from jax.experimental import pallas as pl
from jax.experimental.pallas import tpu as pltpu
from jax.sharding import PartitionSpec as P

KERNEL_NORM = 21.0 / (2.0 * math.pi)
CENTRE = 0.75
CHUNK = 64
LOGICAL = pl.DeviceIdType.LOGICAL
F32 = jnp.float32
BF16 = jnp.bfloat16


def rounded(value):
    return value.astype(BF16).astype(F32)


def three_pieces(value):
    first = rounded(value)
    rest = value - first
    second = rounded(rest)
    return first, second, rest - second


def dot_rows(left, right):
    return lax.dot_general(left, right, (((1,), (1,)), ((), ())), preferred_element_type=F32)


def dot_plain(left, right):
    return lax.dot_general(left, right, (((1,), (0,)), ((), ())), preferred_element_type=F32)


def pair_kernel(
    ring,
    peers,
    cells,
    slots,
    send_s,
    pair_s,
    counts_s,
    send_ref,
    pair_ref,
    pos_ref,
    mass_ref,
    smooth_ref,
    entropy_ref,
    out_ref,
    table,
    table_len,
    table_press,
    table_gap,
    columns,
    fourths,
    aug,
    out_msg,
    in_msg,
    out_press,
    in_press,
    source_rows,
    source_stack,
    dist,
    near_mats,
    far_mats,
    results,
    send_sem,
    recv_sem,
    send_sem2,
    recv_sem2,
    ready_sem,
):
    me = lax.axis_index(("cells", "sub"))
    local_next = cells - 1
    local_own = cells // 2
    local_count = local_next + local_own
    total_count = local_count + peers - 1
    stride = results.shape[0] // 8

    barrier = pltpu.get_barrier_semaphore()
    for step in range(1, ring):
        pl.semaphore_signal(barrier, inc=1, device_id=me ^ step, device_id_type=LOGICAL)
    for step in range(1, peers // ring):
        pl.semaphore_signal(
            barrier, inc=1, device_id=me ^ (ring * step), device_id_type=LOGICAL
        )

    row = lax.broadcasted_iota(jnp.int32, (8, slots), 0)
    upper = row < 4
    weight_row = (row == 3) | (row == 7)
    lane = lax.broadcasted_iota(jnp.int32, (1, slots), 1)

    for cell in range(cells):
        mass_row = jnp.where(lane < counts_s[cell], mass_ref[cell : cell + 1, :], 0.0)
        for half in (0, 4):
            for axis in range(3):
                row_at = half + axis
                table[cell, row_at : row_at + 1, :] = pos_ref[axis, cell : cell + 1, :] - CENTRE
            table[cell, half + 3 : half + 4, :] = mass_row
    table[cells] = jnp.zeros((8, slots), F32)
    for cell in range(cells):
        table_len[cell] = jnp.broadcast_to(smooth_ref[cell : cell + 1, :], (8, slots))
    table_len[cells] = jnp.ones((8, slots), F32)
    table_press[cells] = jnp.zeros((8, slots), F32)
    results[...] = jnp.zeros(results.shape, F32)

    def fill_out(step, carry):
        peer = me ^ step
        chosen = send_s[0, peer]
        first = jnp.where(chosen < 0, cells, chosen)
        second = pair_s[0, peer]
        out_msg[step, 0:8, :] = jnp.where(upper, table[first], table[second])
        out_msg[step, 8:10, :] = jnp.where(row < 1, table_len[first], table_len[second])[0:2, :]
        return carry

    lax.fori_loop(0, peers, fill_out, 0, unroll=4)

    def fill_local(index, first, second):
        in_msg[peers + index, 0:8, :] = jnp.where(upper, table[first], table[second])
        in_msg[peers + index, 8:9, :] = table_len[first, 0:1, :]
        in_msg[peers + index, 9:10, :] = table_len[second, 0:1, :]

    for cell in range(local_next):
        fill_local(cell, cell + 1, cell)
    for turn in range(local_own):
        fill_local(local_next + turn, 2 * turn, 2 * turn + 1)

    blank = jnp.zeros((8, slots), F32)
    for cell in range(cells):
        own = table[cell]
        square = own * own
        total = pltpu.roll(square, 1, 0) + pltpu.roll(square, 2, 0) + pltpu.roll(square, 3, 0)
        own_len = table_len[cell]
        table_gap[cell] = own_len * own_len - total
        p0, p1, p2 = three_pieces(jnp.where(weight_row, total, own))
        one = jnp.ones((8, slots), F32)
        q0 = jnp.where(weight_row, one, -2.0 * p0)
        q1 = jnp.where(weight_row, p0, -2.0 * p1)
        q2 = jnp.where(weight_row, p1, -2.0 * p2)
        q4 = jnp.where(weight_row, p2, -2.0 * p1)
        parts = [jnp.where(upper, q0, q1), jnp.where(upper, q2, q0), jnp.where(upper, q4, q0)]
        aug[cell, 0] = jnp.concatenate(parts + [blank] * 5, axis=0).astype(BF16)
        aug[cell, 1] = jnp.concatenate([blank] * 3 + parts + [blank] * 2, axis=0).astype(BF16)

    pl.semaphore_wait(barrier, ring + peers // ring - 2)
    for step in range(1, ring):
        pl.semaphore_signal(ready_sem, inc=1, device_id=me ^ step, device_id_type=LOGICAL)

    def copy_out(step, source, target, sent, received):
        pltpu.make_async_remote_copy(
            src_ref=source.at[step],
            dst_ref=target.at[step],
            send_sem=sent,
            recv_sem=received.at[(step + 2) // 4],
            device_id=me ^ step,
            device_id_type=LOGICAL,
        ).start()

    def wait_in(group, count, ref, sem):
        got = ref.at[pl.ds(0, count)]
        pltpu.make_async_copy(got, got, sem.at[group]).wait()

    def slot_of(turn):
        return jnp.where(turn < local_count, peers + turn, turn - local_count + 1)

    def targets_of(turn):
        peer = jnp.where(turn < local_count, 0, me ^ (turn - local_count + 1))
        own = 2 * (turn - local_next)
        local_first = jnp.where(turn < local_next, turn, own)
        local_second = jnp.where(turn < local_next, turn + 1, own + 1)
        first = jnp.where(turn < local_count, local_first, pair_s[0, peer])
        second = jnp.where(turn < local_count, local_second, jnp.maximum(send_s[0, peer], 0))
        return first, second

    def stage_distance(turn, half):
        slot = slot_of(turn)
        first, second = targets_of(turn)
        data = in_msg[slot, 0:8, :]
        square = data * data
        total = pltpu.roll(square, 1, 0) + pltpu.roll(square, 2, 0) + pltpu.roll(square, 3, 0)
        p0, p1, p2 = three_pieces(jnp.where(weight_row, total, data))
        o0 = jnp.where(weight_row, 1.0, p0)
        o1 = jnp.where(weight_row, 1.0, p1)
        r0 = pltpu.roll(p0, 4, 0)
        r1 = pltpu.roll(p1, 4, 0)
        r2 = pltpu.roll(p2, 4, 0)
        s0 = pltpu.roll(o0, 4, 0)
        s1 = pltpu.roll(o1, 4, 0)
        far_len = in_msg[slot, 8:10, :]
        masses = jnp.where(row < 3, data[3:4, :], data[7:8, :])
        stack = jnp.concatenate(
            [
                jnp.where(upper, p0, s0),
                jnp.where(upper, o0, r1),
                jnp.where(upper, o1, r2),
                jnp.where(upper, r0, o0),
                jnp.where(upper, s0, p1),
                jnp.where(upper, s1, p2),
                jnp.where(row < 1, far_len[0:1, :], jnp.where(row < 2, far_len[1:2, :], masses)),
                jnp.zeros((8, slots), F32),
            ],
            axis=0,
        )
        turned = jnp.transpose(stack)
        right = jnp.concatenate([aug[first, 0], aug[second, 1]], axis=1)
        dist[half] = dot_plain(turned.astype(BF16), right)
        columns[half] = turned
        weight = jnp.where(upper, data[3:4, :], data[7:8, :])
        rows = weight * jnp.where(weight_row, 1.0, data)
        source_rows[slot] = rows
        m0, m1, m2 = three_pieces(rows)
        v0, v1, v2 = three_pieces(weight * total)
        v1 = pltpu.roll(v1, 7, 0)
        v2 = pltpu.roll(v2, 6, 0)
        squares = jnp.where(weight_row, v0, jnp.where((row == 2) | (row == 6), v1, v2))
        source_stack[half] = jnp.concatenate([m0, m1, m2, squares], axis=0).astype(BF16)

    def split_store(ref, index, block, lanes, value):
        top = value.astype(BF16)
        lanes = slice(lanes, lanes + slots)
        ref[index + (slice(block, block + CHUNK), lanes)] = top
        rest = (value - top.astype(F32)).astype(BF16)
        ref[index + (slice(slots + block, slots + block + CHUNK), lanes)] = rest

    def stage_terms(turn, half):
        slot = slot_of(turn)
        pair_targets = targets_of(turn)
        for side in range(2):
            len_i = table_len[pair_targets[side], 0:1, :]
            fourth = jnp.zeros((8, slots), F32)
            for block in range(0, slots, CHUNK):
                rows = slice(block, block + CHUNK)
                raw = jnp.maximum(dist[half, rows, side * slots : (side + 1) * slots], 1e-30)
                radius = raw * lax.rsqrt(raw)
                t_i = jnp.maximum(len_i - radius, 0.0)
                cube = t_i * t_i * t_i
                t_j = jnp.maximum(columns[half, rows, 48 + side : 49 + side] - radius, 0.0)
                split_store(near_mats, (half,), block, side * slots, cube)
                split_store(far_mats, (slot,), block, side * slots, t_j * t_j * t_j)
                term = cube * t_i * columns[half, rows, 50 + side : 51 + side]
                for at in range(0, CHUNK, 8):
                    fourth = fourth + term[at : at + 8, :]
            for shift in (4, 2, 1):
                fourth = fourth + pltpu.roll(fourth, shift, 0)
            fourths[half, side] = fourth

    def stacked_pieces(value):
        p0, p1, p2 = three_pieces(value)
        stack = jnp.concatenate([p0, p1, p2, jnp.zeros((8, slots), F32)], axis=0).astype(BF16)
        return jnp.concatenate([stack, stack], axis=1)

    def sum_pieces(value):
        return value[0:8, :] + value[8:16, :] + value[16:24, :]

    def target_rows(turn):
        first, second = targets_of(turn)
        return jnp.where(upper, table[first], table[second])

    def moments(first_sums, second_sums, turn):
        sums = jnp.where(upper, first_sums, second_sums)
        weight = jnp.where(upper, first_sums[3:4, :], second_sums[7:8, :])
        return target_rows(turn) * weight - sums

    def stage_sums(turn, half):
        slot = slot_of(turn)
        first, second = targets_of(turn)
        stack = source_stack[half]
        left = jnp.concatenate([stack, stack], axis=1)
        found = dot_plain(left, near_mats[half])

        def piece(at):
            return jnp.where(upper, found[at : at + 8, 0:slots], found[at : at + 8, slots:])

        cubes = piece(0) + piece(8) + piece(16)
        square = piece(24)
        fourth = jnp.where(upper, fourths[half, 0], fourths[half, 1])
        square = square + pltpu.roll(square, 1, 0) + pltpu.roll(square, 2, 0)
        place = jnp.where(upper, table[first], table[second])
        gap = jnp.where(upper, table_gap[first], table_gap[second])
        length = jnp.where(upper, table_len[first], table_len[second])
        weight = jnp.where(upper, cubes[3:4, :], cubes[7:8, :])
        cross = place * cubes
        cross = pltpu.roll(cross, 1, 0) + pltpu.roll(cross, 2, 0) + pltpu.roll(cross, 3, 0)
        dens = gap * weight + 2.0 * cross - square - 0.75 * length * fourth
        slope = place * weight - cubes
        results[pl.ds(slot, 8, stride=stride), :] = jnp.where(weight_row, dens, slope)

    def sums(turn, bank):
        stage_sums(2 * turn, 2 * bank)
        stage_sums(2 * turn + 1, 2 * bank + 1)

    def terms(turn, bank):
        stage_terms(2 * turn, 2 * bank)
        stage_terms(2 * turn + 1, 2 * bank + 1)

    def distances(turn, bank):
        stage_distance(2 * turn, 2 * bank)
        stage_distance(2 * turn + 1, 2 * bank + 1)

    def full_turn(turn, bank):
        sums(turn - 1, 1 - bank)
        terms(turn, bank)
        distances(turn + 1, 1 - bank)

    turns = total_count // 2
    mixed = local_count // 2
    local_steps = (mixed - 2) // 2
    early_steps = 1

    def local_step(step, carry):
        full_turn(2 * step + 1, 1)
        full_turn(2 * step + 2, 0)
        return carry

    def far_step(step, carry):
        turn = 2 * step + mixed
        wait_in(step + 1, 4, in_msg, recv_sem)
        full_turn(turn, mixed % 2)
        full_turn(turn + 1, (mixed + 1) % 2)
        return carry

    distances(0, 0)
    terms(0, 0)
    distances(1, 1)
    lax.fori_loop(0, early_steps, local_step, 0)
    pl.semaphore_wait(ready_sem, ring - 1)

    def send(step, carry):
        copy_out(step, out_msg, in_msg, send_sem, recv_sem)
        return carry

    lax.fori_loop(1, peers, send, 0)
    lax.fori_loop(early_steps, local_steps, local_step, 0)
    for turn in range(2 * local_steps + 1, mixed):
        if turn == mixed - 1:
            wait_in(0, 1, in_msg, recv_sem)
        full_turn(turn, turn % 2)
    steps = (turns - 1 - mixed) // 2
    lax.fori_loop(0, steps, far_step, 0)
    rest = (peers - 2) % 4
    for turn in range(mixed + 2 * steps, turns - 1):
        wait_in(steps + 1, rest, in_msg, recv_sem)
        full_turn(turn, turn % 2)
    sums(turns - 2, turns % 2)
    terms(turns - 1, (turns - 1) % 2)
    sums(turns - 1, (turns - 1) % 2)

    spare = stride - peers
    cell_ids = lax.broadcasted_iota(jnp.int32, (cells, peers), 0)
    extra = lax.broadcasted_iota(jnp.int32, (cells, spare), 1)
    extra_cell = lax.broadcasted_iota(jnp.int32, (cells, spare), 0)
    own_turn = 2 * (extra - local_next)
    is_next = extra < local_next
    is_own = (extra >= local_next) & (extra < local_count)
    extra_first = jnp.where(is_next, extra, jnp.where(is_own, own_turn, -1))
    extra_second = jnp.where(is_next, extra + 1, jnp.where(is_own, own_turn + 1, -1))

    from_peer = lax.broadcasted_iota(jnp.int32, (peers, peers), 0)
    at_step = lax.broadcasted_iota(jnp.int32, (peers, peers), 1)
    order = jnp.where(from_peer == at_step ^ me, 1.0, 0.0).astype(BF16)

    def by_step(keys):
        wide_keys = jnp.broadcast_to(keys.astype(F32), (16, peers)).astype(BF16)
        return dot_plain(wide_keys, order)[0:1, :].astype(jnp.int32)

    def owner(keys, extra_keys):
        near = jnp.where(cell_ids == keys, 1.0, 0.0)
        local = jnp.where(extra_cell == extra_keys, 1.0, 0.0)
        return jnp.concatenate([near, local], axis=1).astype(BF16)

    owner_first = owner(by_step(pair_ref[...]), extra_first)
    owner_second = owner(by_step(send_ref[...]), extra_second)

    owners = jnp.concatenate([owner_first, owner_first, owner_second, owner_second], axis=1)

    def summed(quantity):
        parts = []
        for at in (quantity, quantity + 4):
            value = results[at * stride : (at + 1) * stride, :]
            top = value.astype(BF16)
            parts += [top, (value - top.astype(F32)).astype(BF16)]
        return dot_plain(owners, jnp.concatenate(parts, axis=0))

    lens = smooth_ref[...]
    len2 = lens * lens
    len4 = len2 * len2
    norm = KERNEL_NORM / (len4 * len4)
    cell_row = lax.broadcasted_iota(jnp.int32, (cells, slots), 0)
    limit = jnp.zeros((cells, slots), jnp.int32)
    for cell in range(cells):
        limit = jnp.where(cell_row == cell, counts_s[cell], limit)
    occupied = lax.broadcasted_iota(jnp.int32, (cells, slots), 1) < limit
    total = summed(3) * (4.0 * norm)
    safe = jnp.where(occupied, total, 1.0)
    pressure = entropy_ref[...] * jnp.exp(jnp.log(safe) * (-1.0 / 3.0))
    strength = jnp.where(occupied, pressure * (20.0 * norm), 0.0)
    out_ref[0] = jnp.where(occupied, total, 0.0)
    for cell in range(cells):
        table_press[cell] = jnp.broadcast_to(strength[cell : cell + 1, :], (8, slots))

    def send_press(step, carry):
        peer = me ^ step
        chosen = send_s[0, peer]
        first = jnp.where(chosen < 0, cells, chosen)
        second = pair_s[0, peer]
        out_press[step] = jnp.where(row < 1, table_press[first], table_press[second])[0:2, :]
        copy_out(step, out_press, in_press, send_sem2, recv_sem2)
        return carry

    lax.fori_loop(1, peers, send_press, 0, unroll=2)
    near_part = [summed(axis) * strength for axis in range(3)]

    def fill_press(index, first, second):
        in_press[peers + index, 0:1, :] = table_press[first, 0:1, :]
        in_press[peers + index, 1:2, :] = table_press[second, 0:1, :]

    for cell in range(local_next):
        fill_press(cell, cell + 1, cell)
    for turn in range(local_own):
        fill_press(local_next + turn, 2 * turn, 2 * turn + 1)

    def stage_force(turn):
        slot = slot_of(turn)
        press = jnp.where(upper, in_press[slot, 0:1, :], in_press[slot, 1:2, :])
        found = sum_pieces(dot_plain(stacked_pieces(source_rows[slot] * press), far_mats[slot]))
        slope = moments(found[:, 0:slots], found[:, slots : 2 * slots], turn)
        results[pl.ds(slot, 8, stride=stride), :] = slope

    for turn in range(local_count):
        stage_force(turn)

    def far_force(step, carry):
        for half in range(2):
            wait_in(2 * step + 1 + half, 4, in_press, recv_sem2)
        for at in range(8):
            stage_force(local_count + 1 + 8 * step + at)
        return carry

    wait_in(0, 1, in_press, recv_sem2)
    stage_force(local_count)
    steps = (peers - 2) // 8
    lax.fori_loop(0, steps, far_force, 0)
    tail = local_count + 1 + 8 * steps
    for at in range(tail, total_count, 4):
        wait_in((at - local_count + 3) // 4, min(4, total_count - at), in_press, recv_sem2)
    for at in range(tail, total_count):
        stage_force(at)
    for axis in range(3):
        out_ref[1 + axis] = jnp.where(occupied, near_part[axis] + summed(axis), 0.0)

    def drain(ref, sem):
        moved = ref.at[pl.ds(0, peers - 1)]
        pltpu.make_async_copy(moved, moved, sem).wait()

    drain(out_msg, send_sem)
    drain(out_press, send_sem2)


def split_kernel(found_ref, density_ref, accel_ref):
    density_ref[...] = found_ref[0]
    accel_ref[...] = found_ref[1:4]


def on_device(send_cells, pair_cell, counts, positions, mass, smooth, entropy):
    cells, slots = mass.shape
    peers = lax.axis_size(("cells", "sub"))
    ring = lax.axis_size("sub")
    chosen = send_cells.reshape(1, peers)
    partner = pair_cell.reshape(1, peers)
    stride = peers + 32
    vmem = pl.BlockSpec(memory_space=pltpu.VMEM)
    smem = pl.BlockSpec(memory_space=pltpu.SMEM)
    found = pl.pallas_call(
        functools.partial(pair_kernel, ring, peers, cells, slots),
        out_shape=jax.ShapeDtypeStruct((4, cells, slots), F32),
        in_specs=[smem, smem, smem] + [vmem] * 6,
        out_specs=vmem,
        scratch_shapes=[
            pltpu.VMEM((cells + 1, 8, slots), F32),
            pltpu.VMEM((cells + 1, 8, slots), F32),
            pltpu.VMEM((cells + 1, 8, slots), F32),
            pltpu.VMEM((cells, 8, slots), F32),
            pltpu.VMEM((4, slots, 64), F32),
            pltpu.VMEM((4, 2, 8, slots), F32),
            pltpu.VMEM((cells, 2, 64, slots), BF16),
            pltpu.VMEM((peers, 10, slots), F32),
            pltpu.VMEM((stride, 10, slots), F32),
            pltpu.VMEM((peers, 2, slots), F32),
            pltpu.VMEM((stride, 2, slots), F32),
            pltpu.VMEM((stride, 8, slots), F32),
            pltpu.VMEM((4, 32, slots), BF16),
            pltpu.VMEM((4, slots, 2 * slots), F32),
            pltpu.VMEM((4, 2 * slots, 2 * slots), BF16),
            pltpu.VMEM((stride, 2 * slots, 2 * slots), BF16),
            pltpu.VMEM((8 * stride, slots), F32),
            pltpu.SemaphoreType.DMA,
            pltpu.SemaphoreType.DMA(((peers + 1) // 4 + 1,)),
            pltpu.SemaphoreType.DMA,
            pltpu.SemaphoreType.DMA(((peers + 1) // 4 + 1,)),
            pltpu.SemaphoreType.REGULAR,
        ],
        compiler_params=pltpu.CompilerParams(
            collective_id=0, has_side_effects=True, vmem_limit_bytes=56 * 2**20
        ),
        name="cell_pairs",
    )(chosen, partner, counts, chosen, partner, positions, mass, smooth, entropy)
    return pl.pallas_call(
        split_kernel,
        out_shape=(
            jax.ShapeDtypeStruct((cells, slots), F32),
            jax.ShapeDtypeStruct((3, cells, slots), F32),
        ),
        in_specs=[vmem],
        out_specs=(vmem, vmem),
        name="split_outputs",
    )(found)


def solution(mesh):
    in_specs = (
        P(("cells", "sub"), None, None),
        P(("cells", "sub"), None, None),
        P(("cells", "sub")),
        P(None, ("cells", "sub"), None),
        P(("cells", "sub"), None),
        P(("cells", "sub"), None),
        P(("cells", "sub"), None),
    )
    out_specs = (P(("cells", "sub"), None), P(None, ("cells", "sub"), None))
    return jax.shard_map(
        on_device, mesh=mesh, in_specs=in_specs, out_specs=out_specs, check_vma=False
    )
```

```python
import functools
import math

import jax
import jax.numpy as jnp
from jax import lax
from jax.experimental import pallas as pl
from jax.experimental.pallas import tpu as pltpu
from jax.sharding import PartitionSpec as P

KERNEL_NORM = 21.0 / (2.0 * math.pi)
CENTRE = 0.75
CHUNK = 64
LOGICAL = pl.DeviceIdType.LOGICAL
F32 = jnp.float32
BF16 = jnp.bfloat16


def rounded(value):
    return value.astype(BF16).astype(F32)


def three_pieces(value):
    first = rounded(value)
    rest = value - first
    second = rounded(rest)
    return first, second, rest - second


def dot_rows(left, right):
    return lax.dot_general(left, right, (((1,), (1,)), ((), ())), preferred_element_type=F32)


def dot_plain(left, right):
    return lax.dot_general(left, right, (((1,), (0,)), ((), ())), preferred_element_type=F32)


def pair_kernel(
    ring,
    peers,
    cells,
    slots,
    send_s,
    pair_s,
    counts_s,
    send_ref,
    pair_ref,
    pos_ref,
    mass_ref,
    smooth_ref,
    entropy_ref,
    out_ref,
    table,
    table_len,
    table_press,
    table_gap,
    columns,
    fourths,
    aug,
    out_msg,
    in_msg,
    out_press,
    in_press,
    source_rows,
    source_stack,
    dist,
    near_mats,
    far_mats,
    results,
    send_sem,
    recv_sem,
    send_sem2,
    recv_sem2,
    ready_sem,
):
    me = lax.axis_index(("cells", "sub"))
    local_next = cells - 1
    local_own = cells // 2
    local_count = local_next + local_own
    total_count = local_count + peers - 1
    stride = results.shape[0] // 8

    barrier = pltpu.get_barrier_semaphore()
    for step in range(1, ring):
        pl.semaphore_signal(barrier, inc=1, device_id=me ^ step, device_id_type=LOGICAL)
    for step in range(1, peers // ring):
        pl.semaphore_signal(
            barrier, inc=1, device_id=me ^ (ring * step), device_id_type=LOGICAL
        )

    row = lax.broadcasted_iota(jnp.int32, (8, slots), 0)
    upper = row < 4
    weight_row = (row == 3) | (row == 7)
    lane = lax.broadcasted_iota(jnp.int32, (1, slots), 1)

    for cell in range(cells):
        mass_row = jnp.where(lane < counts_s[cell], mass_ref[cell : cell + 1, :], 0.0)
        for half in (0, 4):
            for axis in range(3):
                row_at = half + axis
                table[cell, row_at : row_at + 1, :] = pos_ref[axis, cell : cell + 1, :] - CENTRE
            table[cell, half + 3 : half + 4, :] = mass_row
    table[cells] = jnp.zeros((8, slots), F32)
    for cell in range(cells):
        table_len[cell] = jnp.broadcast_to(smooth_ref[cell : cell + 1, :], (8, slots))
    table_len[cells] = jnp.ones((8, slots), F32)
    table_press[cells] = jnp.zeros((8, slots), F32)
    results[...] = jnp.zeros(results.shape, F32)

    def fill_out(step, carry):
        peer = me ^ step
        chosen = send_s[0, peer]
        first = jnp.where(chosen < 0, cells, chosen)
        second = pair_s[0, peer]
        out_msg[step, 0:8, :] = jnp.where(upper, table[first], table[second])
        out_msg[step, 8:10, :] = jnp.where(row < 1, table_len[first], table_len[second])[0:2, :]
        return carry

    lax.fori_loop(0, peers, fill_out, 0, unroll=4)

    def fill_local(index, first, second):
        in_msg[peers + index, 0:8, :] = jnp.where(upper, table[first], table[second])
        in_msg[peers + index, 8:9, :] = table_len[first, 0:1, :]
        in_msg[peers + index, 9:10, :] = table_len[second, 0:1, :]

    for cell in range(local_next):
        fill_local(cell, cell + 1, cell)
    for turn in range(local_own):
        fill_local(local_next + turn, 2 * turn, 2 * turn + 1)

    blank = jnp.zeros((8, slots), F32)
    for cell in range(cells):
        own = table[cell]
        square = own * own
        total = pltpu.roll(square, 1, 0) + pltpu.roll(square, 2, 0) + pltpu.roll(square, 3, 0)
        own_len = table_len[cell]
        table_gap[cell] = own_len * own_len - total
        p0, p1, p2 = three_pieces(jnp.where(weight_row, total, own))
        one = jnp.ones((8, slots), F32)
        q0 = jnp.where(weight_row, one, -2.0 * p0)
        q1 = jnp.where(weight_row, p0, -2.0 * p1)
        q2 = jnp.where(weight_row, p1, -2.0 * p2)
        q4 = jnp.where(weight_row, p2, -2.0 * p1)
        parts = [jnp.where(upper, q0, q1), jnp.where(upper, q2, q0), jnp.where(upper, q4, q0)]
        aug[cell, 0] = jnp.concatenate(parts + [blank] * 5, axis=0).astype(BF16)
        aug[cell, 1] = jnp.concatenate([blank] * 3 + parts + [blank] * 2, axis=0).astype(BF16)

    pl.semaphore_wait(barrier, ring + peers // ring - 2)
    for step in range(1, ring):
        pl.semaphore_signal(ready_sem, inc=1, device_id=me ^ step, device_id_type=LOGICAL)

    def copy_out(step, source, target, sent, received):
        pltpu.make_async_remote_copy(
            src_ref=source.at[step],
            dst_ref=target.at[step],
            send_sem=sent,
            recv_sem=received.at[(step + 2) // 4],
            device_id=me ^ step,
            device_id_type=LOGICAL,
        ).start()

    def wait_in(group, count, ref, sem):
        got = ref.at[pl.ds(0, count)]
        pltpu.make_async_copy(got, got, sem.at[group]).wait()

    def slot_of(turn):
        return jnp.where(turn < local_count, peers + turn, turn - local_count + 1)

    def targets_of(turn):
        peer = jnp.where(turn < local_count, 0, me ^ (turn - local_count + 1))
        own = 2 * (turn - local_next)
        local_first = jnp.where(turn < local_next, turn, own)
        local_second = jnp.where(turn < local_next, turn + 1, own + 1)
        first = jnp.where(turn < local_count, local_first, pair_s[0, peer])
        second = jnp.where(turn < local_count, local_second, jnp.maximum(send_s[0, peer], 0))
        return first, second

    def stage_distance(turn, half):
        slot = slot_of(turn)
        first, second = targets_of(turn)
        data = in_msg[slot, 0:8, :]
        square = data * data
        total = pltpu.roll(square, 1, 0) + pltpu.roll(square, 2, 0) + pltpu.roll(square, 3, 0)
        p0, p1, p2 = three_pieces(jnp.where(weight_row, total, data))
        o0 = jnp.where(weight_row, 1.0, p0)
        o1 = jnp.where(weight_row, 1.0, p1)
        r0 = pltpu.roll(p0, 4, 0)
        r1 = pltpu.roll(p1, 4, 0)
        r2 = pltpu.roll(p2, 4, 0)
        s0 = pltpu.roll(o0, 4, 0)
        s1 = pltpu.roll(o1, 4, 0)
        far_len = in_msg[slot, 8:10, :]
        masses = jnp.where(row < 3, data[3:4, :], data[7:8, :])
        stack = jnp.concatenate(
            [
                jnp.where(upper, p0, s0),
                jnp.where(upper, o0, r1),
                jnp.where(upper, o1, r2),
                jnp.where(upper, r0, o0),
                jnp.where(upper, s0, p1),
                jnp.where(upper, s1, p2),
                jnp.where(row < 1, far_len[0:1, :], jnp.where(row < 2, far_len[1:2, :], masses)),
                jnp.zeros((8, slots), F32),
            ],
            axis=0,
        )
        turned = jnp.transpose(stack)
        right = jnp.concatenate([aug[first, 0], aug[second, 1]], axis=1)
        dist[half] = dot_plain(turned.astype(BF16), right)
        columns[half] = turned
        weight = jnp.where(upper, data[3:4, :], data[7:8, :])
        rows = weight * jnp.where(weight_row, 1.0, data)
        source_rows[slot] = rows
        m0, m1, m2 = three_pieces(rows)
        v0, v1, v2 = three_pieces(weight * total)
        v1 = pltpu.roll(v1, 7, 0)
        v2 = pltpu.roll(v2, 6, 0)
        squares = jnp.where(weight_row, v0, jnp.where((row == 2) | (row == 6), v1, v2))
        source_stack[half] = jnp.concatenate([m0, m1, m2, squares], axis=0).astype(BF16)

    def split_store(ref, index, block, lanes, value):
        top = value.astype(BF16)
        lanes = slice(lanes, lanes + slots)
        ref[index + (slice(block, block + CHUNK), lanes)] = top
        rest = (value - top.astype(F32)).astype(BF16)
        ref[index + (slice(slots + block, slots + block + CHUNK), lanes)] = rest

    def stage_terms(turn, half):
        slot = slot_of(turn)
        pair_targets = targets_of(turn)
        for side in range(2):
            len_i = table_len[pair_targets[side], 0:1, :]
            fourth = jnp.zeros((8, slots), F32)
            for block in range(0, slots, CHUNK):
                rows = slice(block, block + CHUNK)
                raw = jnp.maximum(dist[half, rows, side * slots : (side + 1) * slots], 1e-30)
                radius = raw * lax.rsqrt(raw)
                t_i = jnp.maximum(len_i - radius, 0.0)
                cube = t_i * t_i * t_i
                t_j = jnp.maximum(columns[half, rows, 48 + side : 49 + side] - radius, 0.0)
                split_store(near_mats, (half,), block, side * slots, cube)
                split_store(far_mats, (slot,), block, side * slots, t_j * t_j * t_j)
                term = cube * t_i * columns[half, rows, 50 + side : 51 + side]
                for at in range(0, CHUNK, 8):
                    fourth = fourth + term[at : at + 8, :]
            for shift in (4, 2, 1):
                fourth = fourth + pltpu.roll(fourth, shift, 0)
            fourths[half, side] = fourth

    def stacked_pieces(value):
        p0, p1, p2 = three_pieces(value)
        stack = jnp.concatenate([p0, p1, p2, jnp.zeros((8, slots), F32)], axis=0).astype(BF16)
        return jnp.concatenate([stack, stack], axis=1)

    def sum_pieces(value):
        return value[0:8, :] + value[8:16, :] + value[16:24, :]

    def target_rows(turn):
        first, second = targets_of(turn)
        return jnp.where(upper, table[first], table[second])

    def moments(first_sums, second_sums, turn):
        sums = jnp.where(upper, first_sums, second_sums)
        weight = jnp.where(upper, first_sums[3:4, :], second_sums[7:8, :])
        return target_rows(turn) * weight - sums

    def stage_sums(turn, half):
        slot = slot_of(turn)
        first, second = targets_of(turn)
        stack = source_stack[half]
        left = jnp.concatenate([stack, stack], axis=1)
        found = dot_plain(left, near_mats[half])

        def piece(at):
            return jnp.where(upper, found[at : at + 8, 0:slots], found[at : at + 8, slots:])

        cubes = piece(0) + piece(8) + piece(16)
        square = piece(24)
        fourth = jnp.where(upper, fourths[half, 0], fourths[half, 1])
        square = square + pltpu.roll(square, 1, 0) + pltpu.roll(square, 2, 0)
        place = jnp.where(upper, table[first], table[second])
        gap = jnp.where(upper, table_gap[first], table_gap[second])
        length = jnp.where(upper, table_len[first], table_len[second])
        weight = jnp.where(upper, cubes[3:4, :], cubes[7:8, :])
        cross = place * cubes
        cross = pltpu.roll(cross, 1, 0) + pltpu.roll(cross, 2, 0) + pltpu.roll(cross, 3, 0)
        dens = gap * weight + 2.0 * cross - square - 0.75 * length * fourth
        slope = place * weight - cubes
        results[pl.ds(slot, 8, stride=stride), :] = jnp.where(weight_row, dens, slope)

    def sums(turn, bank):
        stage_sums(2 * turn, 2 * bank)
        stage_sums(2 * turn + 1, 2 * bank + 1)

    def terms(turn, bank):
        stage_terms(2 * turn, 2 * bank)
        stage_terms(2 * turn + 1, 2 * bank + 1)

    def distances(turn, bank):
        stage_distance(2 * turn, 2 * bank)
        stage_distance(2 * turn + 1, 2 * bank + 1)

    def full_turn(turn, bank):
        for at in range(2):
            stage_terms(2 * turn + at, 2 * bank + at)
            stage_sums(2 * turn - 2 + at, 2 - 2 * bank + at)
            stage_distance(2 * turn + 2 + at, 2 - 2 * bank + at)

    turns = total_count // 2
    mixed = local_count // 2
    local_steps = (mixed - 2) // 2
    early_steps = 1

    def local_step(step, carry):
        full_turn(2 * step + 1, 1)
        full_turn(2 * step + 2, 0)
        return carry

    def far_step(step, carry):
        turn = 2 * step + mixed
        wait_in(step + 1, 4, in_msg, recv_sem)
        full_turn(turn, mixed % 2)
        full_turn(turn + 1, (mixed + 1) % 2)
        return carry

    distances(0, 0)
    terms(0, 0)
    distances(1, 1)
    lax.fori_loop(0, early_steps, local_step, 0)
    pl.semaphore_wait(ready_sem, ring - 1)

    def send(step, carry):
        copy_out(step, out_msg, in_msg, send_sem, recv_sem)
        return carry

    lax.fori_loop(1, peers, send, 0)
    lax.fori_loop(early_steps, local_steps, local_step, 0)
    for turn in range(2 * local_steps + 1, mixed):
        if turn == mixed - 1:
            wait_in(0, 1, in_msg, recv_sem)
        full_turn(turn, turn % 2)
    steps = (turns - 1 - mixed) // 2
    lax.fori_loop(0, steps, far_step, 0)
    rest = (peers - 2) % 4
    for turn in range(mixed + 2 * steps, turns - 1):
        wait_in(steps + 1, rest, in_msg, recv_sem)
        full_turn(turn, turn % 2)
    sums(turns - 2, turns % 2)
    terms(turns - 1, (turns - 1) % 2)
    sums(turns - 1, (turns - 1) % 2)

    spare = stride - peers
    cell_ids = lax.broadcasted_iota(jnp.int32, (cells, peers), 0)
    extra = lax.broadcasted_iota(jnp.int32, (cells, spare), 1)
    extra_cell = lax.broadcasted_iota(jnp.int32, (cells, spare), 0)
    own_turn = 2 * (extra - local_next)
    is_next = extra < local_next
    is_own = (extra >= local_next) & (extra < local_count)
    extra_first = jnp.where(is_next, extra, jnp.where(is_own, own_turn, -1))
    extra_second = jnp.where(is_next, extra + 1, jnp.where(is_own, own_turn + 1, -1))

    from_peer = lax.broadcasted_iota(jnp.int32, (peers, peers), 0)
    at_step = lax.broadcasted_iota(jnp.int32, (peers, peers), 1)
    order = jnp.where(from_peer == at_step ^ me, 1.0, 0.0).astype(BF16)

    def by_step(keys):
        wide_keys = jnp.broadcast_to(keys.astype(F32), (16, peers)).astype(BF16)
        return dot_plain(wide_keys, order)[0:1, :].astype(jnp.int32)

    def owner(keys, extra_keys):
        near = jnp.where(cell_ids == keys, 1.0, 0.0)
        local = jnp.where(extra_cell == extra_keys, 1.0, 0.0)
        return jnp.concatenate([near, local], axis=1).astype(BF16)

    owner_first = owner(by_step(pair_ref[...]), extra_first)
    owner_second = owner(by_step(send_ref[...]), extra_second)

    owners = jnp.concatenate([owner_first, owner_first, owner_second, owner_second], axis=1)

    def summed(quantity):
        parts = []
        for at in (quantity, quantity + 4):
            value = results[at * stride : (at + 1) * stride, :]
            top = value.astype(BF16)
            parts += [top, (value - top.astype(F32)).astype(BF16)]
        return dot_plain(owners, jnp.concatenate(parts, axis=0))

    lens = smooth_ref[...]
    len2 = lens * lens
    len4 = len2 * len2
    norm = KERNEL_NORM / (len4 * len4)
    cell_row = lax.broadcasted_iota(jnp.int32, (cells, slots), 0)
    limit = jnp.zeros((cells, slots), jnp.int32)
    for cell in range(cells):
        limit = jnp.where(cell_row == cell, counts_s[cell], limit)
    occupied = lax.broadcasted_iota(jnp.int32, (cells, slots), 1) < limit
    total = summed(3) * (4.0 * norm)
    safe = jnp.where(occupied, total, 1.0)
    pressure = entropy_ref[...] * jnp.exp(jnp.log(safe) * (-1.0 / 3.0))
    strength = jnp.where(occupied, pressure * (20.0 * norm), 0.0)
    out_ref[0] = jnp.where(occupied, total, 0.0)
    for cell in range(cells):
        table_press[cell] = jnp.broadcast_to(strength[cell : cell + 1, :], (8, slots))

    def send_press(step, carry):
        peer = me ^ step
        chosen = send_s[0, peer]
        first = jnp.where(chosen < 0, cells, chosen)
        second = pair_s[0, peer]
        out_press[step] = jnp.where(row < 1, table_press[first], table_press[second])[0:2, :]
        copy_out(step, out_press, in_press, send_sem2, recv_sem2)
        return carry

    lax.fori_loop(1, peers, send_press, 0, unroll=2)
    near_part = [summed(axis) * strength for axis in range(3)]

    def fill_press(index, first, second):
        in_press[peers + index, 0:1, :] = table_press[first, 0:1, :]
        in_press[peers + index, 1:2, :] = table_press[second, 0:1, :]

    for cell in range(local_next):
        fill_press(cell, cell + 1, cell)
    for turn in range(local_own):
        fill_press(local_next + turn, 2 * turn, 2 * turn + 1)

    def stage_force(turn):
        slot = slot_of(turn)
        press = jnp.where(upper, in_press[slot, 0:1, :], in_press[slot, 1:2, :])
        found = sum_pieces(dot_plain(stacked_pieces(source_rows[slot] * press), far_mats[slot]))
        slope = moments(found[:, 0:slots], found[:, slots : 2 * slots], turn)
        results[pl.ds(slot, 8, stride=stride), :] = slope

    for turn in range(local_count):
        stage_force(turn)

    def far_force(step, carry):
        for half in range(2):
            wait_in(2 * step + 1 + half, 4, in_press, recv_sem2)
        for at in range(8):
            stage_force(local_count + 1 + 8 * step + at)
        return carry

    wait_in(0, 1, in_press, recv_sem2)
    stage_force(local_count)
    steps = (peers - 2) // 8
    lax.fori_loop(0, steps, far_force, 0)
    tail = local_count + 1 + 8 * steps
    for at in range(tail, total_count, 4):
        wait_in((at - local_count + 3) // 4, min(4, total_count - at), in_press, recv_sem2)
    for at in range(tail, total_count):
        stage_force(at)
    for axis in range(3):
        out_ref[1 + axis] = jnp.where(occupied, near_part[axis] + summed(axis), 0.0)

    def drain(ref, sem):
        moved = ref.at[pl.ds(0, peers - 1)]
        pltpu.make_async_copy(moved, moved, sem).wait()

    drain(out_msg, send_sem)
    drain(out_press, send_sem2)


def split_kernel(found_ref, density_ref, accel_ref):
    density_ref[...] = found_ref[0]
    accel_ref[...] = found_ref[1:4]


def on_device(send_cells, pair_cell, counts, positions, mass, smooth, entropy):
    cells, slots = mass.shape
    peers = lax.axis_size(("cells", "sub"))
    ring = lax.axis_size("sub")
    chosen = send_cells.reshape(1, peers)
    partner = pair_cell.reshape(1, peers)
    stride = peers + 32
    vmem = pl.BlockSpec(memory_space=pltpu.VMEM)
    smem = pl.BlockSpec(memory_space=pltpu.SMEM)
    found = pl.pallas_call(
        functools.partial(pair_kernel, ring, peers, cells, slots),
        out_shape=jax.ShapeDtypeStruct((4, cells, slots), F32),
        in_specs=[smem, smem, smem] + [vmem] * 6,
        out_specs=vmem,
        scratch_shapes=[
            pltpu.VMEM((cells + 1, 8, slots), F32),
            pltpu.VMEM((cells + 1, 8, slots), F32),
            pltpu.VMEM((cells + 1, 8, slots), F32),
            pltpu.VMEM((cells, 8, slots), F32),
            pltpu.VMEM((4, slots, 64), F32),
            pltpu.VMEM((4, 2, 8, slots), F32),
            pltpu.VMEM((cells, 2, 64, slots), BF16),
            pltpu.VMEM((peers, 10, slots), F32),
            pltpu.VMEM((stride, 10, slots), F32),
            pltpu.VMEM((peers, 2, slots), F32),
            pltpu.VMEM((stride, 2, slots), F32),
            pltpu.VMEM((stride, 8, slots), F32),
            pltpu.VMEM((4, 32, slots), BF16),
            pltpu.VMEM((4, slots, 2 * slots), F32),
            pltpu.VMEM((4, 2 * slots, 2 * slots), BF16),
            pltpu.VMEM((stride, 2 * slots, 2 * slots), BF16),
            pltpu.VMEM((8 * stride, slots), F32),
            pltpu.SemaphoreType.DMA,
            pltpu.SemaphoreType.DMA(((peers + 1) // 4 + 1,)),
            pltpu.SemaphoreType.DMA,
            pltpu.SemaphoreType.DMA(((peers + 1) // 4 + 1,)),
            pltpu.SemaphoreType.REGULAR,
        ],
        compiler_params=pltpu.CompilerParams(
            collective_id=0, has_side_effects=True, vmem_limit_bytes=56 * 2**20
        ),
        name="cell_pairs",
    )(chosen, partner, counts, chosen, partner, positions, mass, smooth, entropy)
    return pl.pallas_call(
        split_kernel,
        out_shape=(
            jax.ShapeDtypeStruct((cells, slots), F32),
            jax.ShapeDtypeStruct((3, cells, slots), F32),
        ),
        in_specs=[vmem],
        out_specs=(vmem, vmem),
        name="split_outputs",
    )(found)


def solution(mesh):
    in_specs = (
        P(("cells", "sub"), None, None),
        P(("cells", "sub"), None, None),
        P(("cells", "sub")),
        P(None, ("cells", "sub"), None),
        P(("cells", "sub"), None),
        P(("cells", "sub"), None),
        P(("cells", "sub"), None),
    )
    out_specs = (P(("cells", "sub"), None), P(None, ("cells", "sub"), None))
    return jax.shard_map(
        on_device, mesh=mesh, in_specs=in_specs, out_specs=out_specs, check_vma=False
    )
```

```python
import functools
import math

import jax
import jax.numpy as jnp
from jax import lax
from jax.experimental import pallas as pl
from jax.experimental.pallas import tpu as pltpu
from jax.sharding import PartitionSpec as P

KERNEL_NORM = 21.0 / (2.0 * math.pi)
CENTRE = 0.75
CHUNK = 64
LOGICAL = pl.DeviceIdType.LOGICAL
F32 = jnp.float32
BF16 = jnp.bfloat16


def rounded(value):
    return value.astype(BF16).astype(F32)


def three_pieces(value):
    first = rounded(value)
    rest = value - first
    second = rounded(rest)
    return first, second, rest - second


def dot_rows(left, right):
    return lax.dot_general(left, right, (((1,), (1,)), ((), ())), preferred_element_type=F32)


def dot_plain(left, right):
    return lax.dot_general(left, right, (((1,), (0,)), ((), ())), preferred_element_type=F32)


def pair_kernel(
    ring,
    peers,
    cells,
    slots,
    send_s,
    pair_s,
    counts_s,
    send_ref,
    pair_ref,
    pos_ref,
    mass_ref,
    smooth_ref,
    entropy_ref,
    out_ref,
    table,
    table_len,
    table_press,
    table_gap,
    columns,
    fourths,
    aug,
    out_msg,
    in_msg,
    out_press,
    in_press,
    source_rows,
    source_stack,
    dist,
    near_mats,
    far_mats,
    results,
    send_sem,
    recv_sem,
    send_sem2,
    recv_sem2,
    ready_sem,
):
    me = lax.axis_index(("cells", "sub"))
    local_next = cells - 1
    local_own = cells // 2
    local_count = local_next + local_own
    total_count = local_count + peers - 1
    stride = results.shape[0] // 8

    barrier = pltpu.get_barrier_semaphore()
    for step in range(1, ring):
        pl.semaphore_signal(barrier, inc=1, device_id=me ^ step, device_id_type=LOGICAL)
    for step in range(1, peers // ring):
        pl.semaphore_signal(
            barrier, inc=1, device_id=me ^ (ring * step), device_id_type=LOGICAL
        )

    row = lax.broadcasted_iota(jnp.int32, (8, slots), 0)
    upper = row < 4
    weight_row = (row == 3) | (row == 7)
    lane = lax.broadcasted_iota(jnp.int32, (1, slots), 1)

    for cell in range(cells):
        mass_row = jnp.where(lane < counts_s[cell], mass_ref[cell : cell + 1, :], 0.0)
        for half in (0, 4):
            for axis in range(3):
                row_at = half + axis
                table[cell, row_at : row_at + 1, :] = pos_ref[axis, cell : cell + 1, :] - CENTRE
            table[cell, half + 3 : half + 4, :] = mass_row
    table[cells] = jnp.zeros((8, slots), F32)
    for cell in range(cells):
        table_len[cell] = jnp.broadcast_to(smooth_ref[cell : cell + 1, :], (8, slots))
    table_len[cells] = jnp.ones((8, slots), F32)
    table_press[cells] = jnp.zeros((8, slots), F32)
    results[...] = jnp.zeros(results.shape, F32)

    def fill_out(step, carry):
        peer = me ^ step
        chosen = send_s[0, peer]
        first = jnp.where(chosen < 0, cells, chosen)
        second = pair_s[0, peer]
        out_msg[step, 0:8, :] = jnp.where(upper, table[first], table[second])
        out_msg[step, 8:10, :] = jnp.where(row < 1, table_len[first], table_len[second])[0:2, :]
        return carry

    lax.fori_loop(0, peers, fill_out, 0, unroll=4)

    def fill_local(index, first, second):
        in_msg[peers + index, 0:8, :] = jnp.where(upper, table[first], table[second])
        in_msg[peers + index, 8:9, :] = table_len[first, 0:1, :]
        in_msg[peers + index, 9:10, :] = table_len[second, 0:1, :]

    for cell in range(local_next):
        fill_local(cell, cell + 1, cell)
    for turn in range(local_own):
        fill_local(local_next + turn, 2 * turn, 2 * turn + 1)

    blank = jnp.zeros((8, slots), F32)
    for cell in range(cells):
        own = table[cell]
        square = own * own
        total = pltpu.roll(square, 1, 0) + pltpu.roll(square, 2, 0) + pltpu.roll(square, 3, 0)
        own_len = table_len[cell]
        table_gap[cell] = own_len * own_len - total
        p0, p1, p2 = three_pieces(jnp.where(weight_row, total, own))
        one = jnp.ones((8, slots), F32)
        q0 = jnp.where(weight_row, one, -2.0 * p0)
        q1 = jnp.where(weight_row, p0, -2.0 * p1)
        q2 = jnp.where(weight_row, p1, -2.0 * p2)
        q4 = jnp.where(weight_row, p2, -2.0 * p1)
        parts = [jnp.where(upper, q0, q1), jnp.where(upper, q2, q0), jnp.where(upper, q4, q0)]
        aug[cell, 0] = jnp.concatenate(parts + [blank] * 5, axis=0).astype(BF16)
        aug[cell, 1] = jnp.concatenate([blank] * 3 + parts + [blank] * 2, axis=0).astype(BF16)

    pl.semaphore_wait(barrier, ring + peers // ring - 2)
    for step in range(1, ring):
        pl.semaphore_signal(ready_sem, inc=1, device_id=me ^ step, device_id_type=LOGICAL)

    def copy_out(step, source, target, sent, received):
        pltpu.make_async_remote_copy(
            src_ref=source.at[step],
            dst_ref=target.at[step],
            send_sem=sent,
            recv_sem=received.at[(step + 2) // 4],
            device_id=me ^ step,
            device_id_type=LOGICAL,
        ).start()

    def wait_in(group, count, ref, sem):
        got = ref.at[pl.ds(0, count)]
        pltpu.make_async_copy(got, got, sem.at[group]).wait()

    def slot_of(turn):
        return jnp.where(turn < local_count, peers + turn, turn - local_count + 1)

    def targets_of(turn):
        peer = jnp.where(turn < local_count, 0, me ^ (turn - local_count + 1))
        own = 2 * (turn - local_next)
        local_first = jnp.where(turn < local_next, turn, own)
        local_second = jnp.where(turn < local_next, turn + 1, own + 1)
        first = jnp.where(turn < local_count, local_first, pair_s[0, peer])
        second = jnp.where(turn < local_count, local_second, jnp.maximum(send_s[0, peer], 0))
        return first, second

    def stage_distance(turn, half):
        slot = slot_of(turn)
        first, second = targets_of(turn)
        data = in_msg[slot, 0:8, :]
        square = data * data
        total = pltpu.roll(square, 1, 0) + pltpu.roll(square, 2, 0) + pltpu.roll(square, 3, 0)
        p0, p1, p2 = three_pieces(jnp.where(weight_row, total, data))
        o0 = jnp.where(weight_row, 1.0, p0)
        o1 = jnp.where(weight_row, 1.0, p1)
        r0 = pltpu.roll(p0, 4, 0)
        r1 = pltpu.roll(p1, 4, 0)
        r2 = pltpu.roll(p2, 4, 0)
        s0 = pltpu.roll(o0, 4, 0)
        s1 = pltpu.roll(o1, 4, 0)
        far_len = in_msg[slot, 8:10, :]
        masses = jnp.where(row < 3, data[3:4, :], data[7:8, :])
        stack = jnp.concatenate(
            [
                jnp.where(upper, p0, s0),
                jnp.where(upper, o0, r1),
                jnp.where(upper, o1, r2),
                jnp.where(upper, r0, o0),
                jnp.where(upper, s0, p1),
                jnp.where(upper, s1, p2),
                jnp.where(row < 1, far_len[0:1, :], jnp.where(row < 2, far_len[1:2, :], masses)),
                jnp.zeros((8, slots), F32),
            ],
            axis=0,
        )
        turned = jnp.transpose(stack)
        right = jnp.concatenate([aug[first, 0], aug[second, 1]], axis=1)
        dist[half] = dot_plain(turned.astype(BF16), right)
        columns[half] = turned
        weight = jnp.where(upper, data[3:4, :], data[7:8, :])
        rows = weight * jnp.where(weight_row, 1.0, data)
        source_rows[slot] = rows
        m0, m1, m2 = three_pieces(rows)
        v0, v1, v2 = three_pieces(weight * total)
        v1 = pltpu.roll(v1, 7, 0)
        v2 = pltpu.roll(v2, 6, 0)
        squares = jnp.where(weight_row, v0, jnp.where((row == 2) | (row == 6), v1, v2))
        source_stack[half] = jnp.concatenate([m0, m1, m2, squares], axis=0).astype(BF16)

    def split_store(ref, index, block, lanes, value):
        top = value.astype(BF16)
        lanes = slice(lanes, lanes + slots)
        ref[index + (slice(block, block + CHUNK), lanes)] = top
        rest = (value - top.astype(F32)).astype(BF16)
        ref[index + (slice(slots + block, slots + block + CHUNK), lanes)] = rest

    def stage_terms(turn, half):
        slot = slot_of(turn)
        pair_targets = targets_of(turn)
        for side in range(2):
            len_i = table_len[pair_targets[side], 0:1, :]
            fourth = jnp.zeros((8, slots), F32)
            for block in range(0, slots, CHUNK):
                rows = slice(block, block + CHUNK)
                raw = jnp.maximum(dist[half, rows, side * slots : (side + 1) * slots], 1e-30)
                radius = raw * lax.rsqrt(raw)
                t_i = jnp.maximum(len_i - radius, 0.0)
                cube = t_i * t_i * t_i
                t_j = jnp.maximum(columns[half, rows, 48 + side : 49 + side] - radius, 0.0)
                split_store(near_mats, (half,), block, side * slots, cube)
                split_store(far_mats, (slot,), block, side * slots, t_j * t_j * t_j)
                term = cube * t_i * columns[half, rows, 50 + side : 51 + side]
                for at in range(0, CHUNK, 8):
                    fourth = fourth + term[at : at + 8, :]
            for shift in (4, 2, 1):
                fourth = fourth + pltpu.roll(fourth, shift, 0)
            fourths[half, side] = fourth

    def stacked_pieces(value):
        p0, p1, p2 = three_pieces(value)
        stack = jnp.concatenate([p0, p1, p2, jnp.zeros((8, slots), F32)], axis=0).astype(BF16)
        return jnp.concatenate([stack, stack], axis=1)

    def sum_pieces(value):
        return value[0:8, :] + value[8:16, :] + value[16:24, :]

    def target_rows(turn):
        first, second = targets_of(turn)
        return jnp.where(upper, table[first], table[second])

    def moments(first_sums, second_sums, turn):
        sums = jnp.where(upper, first_sums, second_sums)
        weight = jnp.where(upper, first_sums[3:4, :], second_sums[7:8, :])
        return target_rows(turn) * weight - sums

    def stage_sums(turn, half):
        slot = slot_of(turn)
        first, second = targets_of(turn)
        stack = source_stack[half]
        left = jnp.concatenate([stack, stack], axis=1)
        found = dot_plain(left, near_mats[half])

        def piece(at):
            return jnp.where(upper, found[at : at + 8, 0:slots], found[at : at + 8, slots:])

        cubes = piece(0) + piece(8) + piece(16)
        square = piece(24)
        fourth = jnp.where(upper, fourths[half, 0], fourths[half, 1])
        square = square + pltpu.roll(square, 1, 0) + pltpu.roll(square, 2, 0)
        place = jnp.where(upper, table[first], table[second])
        gap = jnp.where(upper, table_gap[first], table_gap[second])
        length = jnp.where(upper, table_len[first], table_len[second])
        weight = jnp.where(upper, cubes[3:4, :], cubes[7:8, :])
        cross = place * cubes
        cross = pltpu.roll(cross, 1, 0) + pltpu.roll(cross, 2, 0) + pltpu.roll(cross, 3, 0)
        dens = gap * weight + 2.0 * cross - square - 0.75 * length * fourth
        slope = place * weight - cubes
        results[pl.ds(slot, 8, stride=stride), :] = jnp.where(weight_row, dens, slope)

    def sums(turn, bank):
        stage_sums(2 * turn, 2 * bank)
        stage_sums(2 * turn + 1, 2 * bank + 1)

    def terms(turn, bank):
        stage_terms(2 * turn, 2 * bank)
        stage_terms(2 * turn + 1, 2 * bank + 1)

    def distances(turn, bank):
        stage_distance(2 * turn, 2 * bank)
        stage_distance(2 * turn + 1, 2 * bank + 1)

    def full_turn(turn, bank):
        for at in range(2):
            stage_terms(2 * turn + at, 2 * bank + at)
            stage_sums(2 * turn - 2 + at, 2 - 2 * bank + at)
            stage_distance(2 * turn + 2 + at, 2 - 2 * bank + at)

    turns = total_count // 2
    mixed = local_count // 2
    local_steps = (mixed - 2) // 2
    early_steps = 1

    def local_step(step, carry):
        full_turn(2 * step + 1, 1)
        full_turn(2 * step + 2, 0)
        return carry

    def far_step(step, carry):
        turn = 2 * step + mixed
        wait_in(step + 1, 4, in_msg, recv_sem)
        full_turn(turn, mixed % 2)
        full_turn(turn + 1, (mixed + 1) % 2)
        return carry

    distances(0, 0)
    terms(0, 0)
    distances(1, 1)
    lax.fori_loop(0, early_steps, local_step, 0)
    pl.semaphore_wait(ready_sem, ring - 1)

    def send(step, carry):
        copy_out(step, out_msg, in_msg, send_sem, recv_sem)
        return carry

    lax.fori_loop(1, peers, send, 0)
    lax.fori_loop(early_steps, local_steps, local_step, 0)
    for turn in range(2 * local_steps + 1, mixed):
        if turn == mixed - 1:
            wait_in(0, 1, in_msg, recv_sem)
        full_turn(turn, turn % 2)
    steps = (turns - 1 - mixed) // 2
    lax.fori_loop(0, steps, far_step, 0)
    rest = (peers - 2) % 4
    for turn in range(mixed + 2 * steps, turns - 1):
        wait_in(steps + 1, rest, in_msg, recv_sem)
        full_turn(turn, turn % 2)
    sums(turns - 2, turns % 2)
    terms(turns - 1, (turns - 1) % 2)
    sums(turns - 1, (turns - 1) % 2)

    spare = stride - peers
    cell_ids = lax.broadcasted_iota(jnp.int32, (cells, peers), 0)
    extra = lax.broadcasted_iota(jnp.int32, (cells, spare), 1)
    extra_cell = lax.broadcasted_iota(jnp.int32, (cells, spare), 0)
    own_turn = 2 * (extra - local_next)
    is_next = extra < local_next
    is_own = (extra >= local_next) & (extra < local_count)
    extra_first = jnp.where(is_next, extra, jnp.where(is_own, own_turn, -1))
    extra_second = jnp.where(is_next, extra + 1, jnp.where(is_own, own_turn + 1, -1))

    from_peer = lax.broadcasted_iota(jnp.int32, (peers, peers), 0)
    at_step = lax.broadcasted_iota(jnp.int32, (peers, peers), 1)
    order = jnp.where(from_peer == at_step ^ me, 1.0, 0.0).astype(BF16)

    def by_step(keys):
        wide_keys = jnp.broadcast_to(keys.astype(F32), (16, peers)).astype(BF16)
        return dot_plain(wide_keys, order)[0:1, :].astype(jnp.int32)

    def owner(keys, extra_keys):
        near = jnp.where(cell_ids == keys, 1.0, 0.0)
        local = jnp.where(extra_cell == extra_keys, 1.0, 0.0)
        return jnp.concatenate([near, local], axis=1).astype(BF16)

    owner_first = owner(by_step(pair_ref[...]), extra_first)
    owner_second = owner(by_step(send_ref[...]), extra_second)

    owners = jnp.concatenate([owner_first, owner_first, owner_second, owner_second], axis=1)

    def summed(quantity):
        parts = []
        for at in (quantity, quantity + 4):
            value = results[at * stride : (at + 1) * stride, :]
            top = value.astype(BF16)
            parts += [top, (value - top.astype(F32)).astype(BF16)]
        return dot_plain(owners, jnp.concatenate(parts, axis=0))

    lens = smooth_ref[...]
    len2 = lens * lens
    len4 = len2 * len2
    norm = KERNEL_NORM / (len4 * len4)
    cell_row = lax.broadcasted_iota(jnp.int32, (cells, slots), 0)
    limit = jnp.zeros((cells, slots), jnp.int32)
    for cell in range(cells):
        limit = jnp.where(cell_row == cell, counts_s[cell], limit)
    occupied = lax.broadcasted_iota(jnp.int32, (cells, slots), 1) < limit
    total = summed(3) * (4.0 * norm)
    safe = jnp.where(occupied, total, 1.0)
    pressure = entropy_ref[...] * jnp.exp(jnp.log(safe) * (-1.0 / 3.0))
    strength = jnp.where(occupied, pressure * (20.0 * norm), 0.0)
    out_ref[0] = jnp.where(occupied, total, 0.0)
    for cell in range(cells):
        table_press[cell] = jnp.broadcast_to(strength[cell : cell + 1, :], (8, slots))

    def send_press(step, carry):
        peer = me ^ step
        chosen = send_s[0, peer]
        first = jnp.where(chosen < 0, cells, chosen)
        second = pair_s[0, peer]
        out_press[step] = jnp.where(row < 1, table_press[first], table_press[second])[0:2, :]
        copy_out(step, out_press, in_press, send_sem2, recv_sem2)
        return carry

    lax.fori_loop(1, peers, send_press, 0, unroll=2)
    near_part = [summed(axis) * strength for axis in range(3)]

    def fill_press(index, first, second):
        in_press[peers + index, 0:1, :] = table_press[first, 0:1, :]
        in_press[peers + index, 1:2, :] = table_press[second, 0:1, :]

    for cell in range(local_next):
        fill_press(cell, cell + 1, cell)
    for turn in range(local_own):
        fill_press(local_next + turn, 2 * turn, 2 * turn + 1)

    def stage_force(turn):
        slot = slot_of(turn)
        press = jnp.where(upper, in_press[slot, 0:1, :], in_press[slot, 1:2, :])
        found = sum_pieces(dot_plain(stacked_pieces(source_rows[slot] * press), far_mats[slot]))
        slope = moments(found[:, 0:slots], found[:, slots : 2 * slots], turn)
        results[pl.ds(slot, 8, stride=stride), :] = slope

    for turn in range(local_count):
        stage_force(turn)

    def far_force(step, carry):
        for half in range(4):
            wait_in(4 * step + 1 + half, 4, in_press, recv_sem2)
        for at in range(16):
            stage_force(local_count + 1 + 16 * step + at)
        return carry

    wait_in(0, 1, in_press, recv_sem2)
    stage_force(local_count)
    steps = (peers - 2) // 16
    lax.fori_loop(0, steps, far_force, 0)
    tail = local_count + 1 + 16 * steps
    for at in range(tail, total_count, 4):
        wait_in((at - local_count + 3) // 4, min(4, total_count - at), in_press, recv_sem2)
    for at in range(tail, total_count):
        stage_force(at)
    for axis in range(3):
        out_ref[1 + axis] = jnp.where(occupied, near_part[axis] + summed(axis), 0.0)

    def drain(ref, sem):
        moved = ref.at[pl.ds(0, peers - 1)]
        pltpu.make_async_copy(moved, moved, sem).wait()

    drain(out_msg, send_sem)
    drain(out_press, send_sem2)


def split_kernel(found_ref, density_ref, accel_ref):
    density_ref[...] = found_ref[0]
    accel_ref[...] = found_ref[1:4]


def on_device(send_cells, pair_cell, counts, positions, mass, smooth, entropy):
    cells, slots = mass.shape
    peers = lax.axis_size(("cells", "sub"))
    ring = lax.axis_size("sub")
    chosen = send_cells.reshape(1, peers)
    partner = pair_cell.reshape(1, peers)
    stride = peers + 32
    vmem = pl.BlockSpec(memory_space=pltpu.VMEM)
    smem = pl.BlockSpec(memory_space=pltpu.SMEM)
    found = pl.pallas_call(
        functools.partial(pair_kernel, ring, peers, cells, slots),
        out_shape=jax.ShapeDtypeStruct((4, cells, slots), F32),
        in_specs=[smem, smem, smem] + [vmem] * 6,
        out_specs=vmem,
        scratch_shapes=[
            pltpu.VMEM((cells + 1, 8, slots), F32),
            pltpu.VMEM((cells + 1, 8, slots), F32),
            pltpu.VMEM((cells + 1, 8, slots), F32),
            pltpu.VMEM((cells, 8, slots), F32),
            pltpu.VMEM((4, slots, 64), F32),
            pltpu.VMEM((4, 2, 8, slots), F32),
            pltpu.VMEM((cells, 2, 64, slots), BF16),
            pltpu.VMEM((peers, 10, slots), F32),
            pltpu.VMEM((stride, 10, slots), F32),
            pltpu.VMEM((peers, 2, slots), F32),
            pltpu.VMEM((stride, 2, slots), F32),
            pltpu.VMEM((stride, 8, slots), F32),
            pltpu.VMEM((4, 32, slots), BF16),
            pltpu.VMEM((4, slots, 2 * slots), F32),
            pltpu.VMEM((4, 2 * slots, 2 * slots), BF16),
            pltpu.VMEM((stride, 2 * slots, 2 * slots), BF16),
            pltpu.VMEM((8 * stride, slots), F32),
            pltpu.SemaphoreType.DMA,
            pltpu.SemaphoreType.DMA(((peers + 1) // 4 + 1,)),
            pltpu.SemaphoreType.DMA,
            pltpu.SemaphoreType.DMA(((peers + 1) // 4 + 1,)),
            pltpu.SemaphoreType.REGULAR,
        ],
        compiler_params=pltpu.CompilerParams(
            collective_id=0, has_side_effects=True, vmem_limit_bytes=56 * 2**20
        ),
        name="cell_pairs",
    )(chosen, partner, counts, chosen, partner, positions, mass, smooth, entropy)
    return pl.pallas_call(
        split_kernel,
        out_shape=(
            jax.ShapeDtypeStruct((cells, slots), F32),
            jax.ShapeDtypeStruct((3, cells, slots), F32),
        ),
        in_specs=[vmem],
        out_specs=(vmem, vmem),
        name="split_outputs",
    )(found)


def solution(mesh):
    in_specs = (
        P(("cells", "sub"), None, None),
        P(("cells", "sub"), None, None),
        P(("cells", "sub")),
        P(None, ("cells", "sub"), None),
        P(("cells", "sub"), None),
        P(("cells", "sub"), None),
        P(("cells", "sub"), None),
    )
    out_specs = (P(("cells", "sub"), None), P(None, ("cells", "sub"), None))
    return jax.shard_map(
        on_device, mesh=mesh, in_specs=in_specs, out_specs=out_specs, check_vma=False
    )
```

```python
import functools
import math

import jax
import jax.numpy as jnp
from jax import lax
from jax.experimental import pallas as pl
from jax.experimental.pallas import tpu as pltpu
from jax.sharding import PartitionSpec as P

KERNEL_NORM = 21.0 / (2.0 * math.pi)
CENTRE = 0.75
CHUNK = 64
LOGICAL = pl.DeviceIdType.LOGICAL
F32 = jnp.float32
BF16 = jnp.bfloat16


def rounded(value):
    return value.astype(BF16).astype(F32)


def three_pieces(value):
    first = rounded(value)
    rest = value - first
    second = rounded(rest)
    return first, second, rest - second


def dot_rows(left, right):
    return lax.dot_general(left, right, (((1,), (1,)), ((), ())), preferred_element_type=F32)


def dot_plain(left, right):
    return lax.dot_general(left, right, (((1,), (0,)), ((), ())), preferred_element_type=F32)


def pair_kernel(
    ring,
    peers,
    cells,
    slots,
    send_s,
    pair_s,
    counts_s,
    send_ref,
    pair_ref,
    pos_ref,
    mass_ref,
    smooth_ref,
    entropy_ref,
    out_ref,
    table,
    table_len,
    table_press,
    table_gap,
    columns,
    fourths,
    aug,
    out_msg,
    in_msg,
    out_press,
    in_press,
    source_rows,
    source_stack,
    dist,
    near_mats,
    far_mats,
    results,
    send_sem,
    recv_sem,
    send_sem2,
    recv_sem2,
    ready_sem,
):
    me = lax.axis_index(("cells", "sub"))
    local_next = cells - 1
    local_own = cells // 2
    local_count = local_next + local_own
    total_count = local_count + peers - 1
    stride = results.shape[0] // 8

    barrier = pltpu.get_barrier_semaphore()
    for step in range(1, ring):
        pl.semaphore_signal(barrier, inc=1, device_id=me ^ step, device_id_type=LOGICAL)
    for step in range(1, peers // ring):
        pl.semaphore_signal(
            barrier, inc=1, device_id=me ^ (ring * step), device_id_type=LOGICAL
        )

    row = lax.broadcasted_iota(jnp.int32, (8, slots), 0)
    upper = row < 4
    weight_row = (row == 3) | (row == 7)
    lane = lax.broadcasted_iota(jnp.int32, (1, slots), 1)

    for cell in range(cells):
        mass_row = jnp.where(lane < counts_s[cell], mass_ref[cell : cell + 1, :], 0.0)
        for half in (0, 4):
            for axis in range(3):
                row_at = half + axis
                table[cell, row_at : row_at + 1, :] = pos_ref[axis, cell : cell + 1, :] - CENTRE
            table[cell, half + 3 : half + 4, :] = mass_row
    table[cells] = jnp.zeros((8, slots), F32)
    for cell in range(cells):
        table_len[cell] = jnp.broadcast_to(smooth_ref[cell : cell + 1, :], (8, slots))
    table_len[cells] = jnp.ones((8, slots), F32)
    table_press[cells] = jnp.zeros((8, slots), F32)
    results[...] = jnp.zeros(results.shape, F32)

    def fill_out(step, carry):
        peer = me ^ step
        chosen = send_s[0, peer]
        first = jnp.where(chosen < 0, cells, chosen)
        second = pair_s[0, peer]
        out_msg[step, 0:8, :] = jnp.where(upper, table[first], table[second])
        out_msg[step, 8:10, :] = jnp.where(row < 1, table_len[first], table_len[second])[0:2, :]
        return carry

    lax.fori_loop(0, peers, fill_out, 0, unroll=4)

    def fill_local(index, first, second):
        in_msg[peers + index, 0:8, :] = jnp.where(upper, table[first], table[second])
        in_msg[peers + index, 8:9, :] = table_len[first, 0:1, :]
        in_msg[peers + index, 9:10, :] = table_len[second, 0:1, :]

    for cell in range(local_next):
        fill_local(cell, cell + 1, cell)
    for turn in range(local_own):
        fill_local(local_next + turn, 2 * turn, 2 * turn + 1)

    blank = jnp.zeros((8, slots), F32)
    for cell in range(cells):
        own = table[cell]
        square = own * own
        total = pltpu.roll(square, 1, 0) + pltpu.roll(square, 2, 0) + pltpu.roll(square, 3, 0)
        own_len = table_len[cell]
        table_gap[cell] = own_len * own_len - total
        p0, p1, p2 = three_pieces(jnp.where(weight_row, total, own))
        one = jnp.ones((8, slots), F32)
        q0 = jnp.where(weight_row, one, -2.0 * p0)
        q1 = jnp.where(weight_row, p0, -2.0 * p1)
        q2 = jnp.where(weight_row, p1, -2.0 * p2)
        q4 = jnp.where(weight_row, p2, -2.0 * p1)
        parts = [jnp.where(upper, q0, q1), jnp.where(upper, q2, q0), jnp.where(upper, q4, q0)]
        aug[cell, 0] = jnp.concatenate(parts + [blank] * 5, axis=0).astype(BF16)
        aug[cell, 1] = jnp.concatenate([blank] * 3 + parts + [blank] * 2, axis=0).astype(BF16)

    spare = stride - peers
    cell_ids = lax.broadcasted_iota(jnp.int32, (cells, peers), 0)
    extra = lax.broadcasted_iota(jnp.int32, (cells, spare), 1)
    extra_cell = lax.broadcasted_iota(jnp.int32, (cells, spare), 0)
    own_turn = 2 * (extra - local_next)
    is_next = extra < local_next
    is_own = (extra >= local_next) & (extra < local_count)
    extra_first = jnp.where(is_next, extra, jnp.where(is_own, own_turn, -1))
    extra_second = jnp.where(is_next, extra + 1, jnp.where(is_own, own_turn + 1, -1))

    from_peer = lax.broadcasted_iota(jnp.int32, (peers, peers), 0)
    at_step = lax.broadcasted_iota(jnp.int32, (peers, peers), 1)
    order = jnp.where(from_peer == at_step ^ me, 1.0, 0.0).astype(BF16)

    def by_step(keys):
        wide_keys = jnp.broadcast_to(keys.astype(F32), (16, peers)).astype(BF16)
        return dot_plain(wide_keys, order)[0:1, :].astype(jnp.int32)

    def owner(keys, extra_keys):
        near = jnp.where(cell_ids == keys, 1.0, 0.0)
        local = jnp.where(extra_cell == extra_keys, 1.0, 0.0)
        return jnp.concatenate([near, local], axis=1).astype(BF16)

    owner_first = owner(by_step(pair_ref[...]), extra_first)
    owner_second = owner(by_step(send_ref[...]), extra_second)

    owners = jnp.concatenate([owner_first, owner_first, owner_second, owner_second], axis=1)

    lens = smooth_ref[...]
    len2 = lens * lens
    len4 = len2 * len2
    norm = KERNEL_NORM / (len4 * len4)
    cell_row = lax.broadcasted_iota(jnp.int32, (cells, slots), 0)
    limit = jnp.zeros((cells, slots), jnp.int32)
    for cell in range(cells):
        limit = jnp.where(cell_row == cell, counts_s[cell], limit)
    occupied = lax.broadcasted_iota(jnp.int32, (cells, slots), 1) < limit

    pl.semaphore_wait(barrier, ring + peers // ring - 2)
    for step in range(1, ring):
        pl.semaphore_signal(ready_sem, inc=1, device_id=me ^ step, device_id_type=LOGICAL)

    def copy_out(step, source, target, sent, received):
        pltpu.make_async_remote_copy(
            src_ref=source.at[step],
            dst_ref=target.at[step],
            send_sem=sent,
            recv_sem=received.at[(step + 2) // 4],
            device_id=me ^ step,
            device_id_type=LOGICAL,
        ).start()

    def wait_in(group, count, ref, sem):
        got = ref.at[pl.ds(0, count)]
        pltpu.make_async_copy(got, got, sem.at[group]).wait()

    def slot_of(turn):
        return jnp.where(turn < local_count, peers + turn, turn - local_count + 1)

    def targets_of(turn):
        peer = jnp.where(turn < local_count, 0, me ^ (turn - local_count + 1))
        own = 2 * (turn - local_next)
        local_first = jnp.where(turn < local_next, turn, own)
        local_second = jnp.where(turn < local_next, turn + 1, own + 1)
        first = jnp.where(turn < local_count, local_first, pair_s[0, peer])
        second = jnp.where(turn < local_count, local_second, jnp.maximum(send_s[0, peer], 0))
        return first, second

    def stage_distance(turn, half):
        slot = slot_of(turn)
        first, second = targets_of(turn)
        data = in_msg[slot, 0:8, :]
        square = data * data
        total = pltpu.roll(square, 1, 0) + pltpu.roll(square, 2, 0) + pltpu.roll(square, 3, 0)
        p0, p1, p2 = three_pieces(jnp.where(weight_row, total, data))
        o0 = jnp.where(weight_row, 1.0, p0)
        o1 = jnp.where(weight_row, 1.0, p1)
        r0 = pltpu.roll(p0, 4, 0)
        r1 = pltpu.roll(p1, 4, 0)
        r2 = pltpu.roll(p2, 4, 0)
        s0 = pltpu.roll(o0, 4, 0)
        s1 = pltpu.roll(o1, 4, 0)
        far_len = in_msg[slot, 8:10, :]
        masses = jnp.where(row < 3, data[3:4, :], data[7:8, :])
        stack = jnp.concatenate(
            [
                jnp.where(upper, p0, s0),
                jnp.where(upper, o0, r1),
                jnp.where(upper, o1, r2),
                jnp.where(upper, r0, o0),
                jnp.where(upper, s0, p1),
                jnp.where(upper, s1, p2),
                jnp.where(row < 1, far_len[0:1, :], jnp.where(row < 2, far_len[1:2, :], masses)),
                jnp.zeros((8, slots), F32),
            ],
            axis=0,
        )
        turned = jnp.transpose(stack)
        right = jnp.concatenate([aug[first, 0], aug[second, 1]], axis=1)
        dist[half] = dot_plain(turned.astype(BF16), right)
        columns[half] = turned
        weight = jnp.where(upper, data[3:4, :], data[7:8, :])
        rows = weight * jnp.where(weight_row, 1.0, data)
        source_rows[slot] = rows
        m0, m1, m2 = three_pieces(rows)
        v0, v1, v2 = three_pieces(weight * total)
        v1 = pltpu.roll(v1, 7, 0)
        v2 = pltpu.roll(v2, 6, 0)
        squares = jnp.where(weight_row, v0, jnp.where((row == 2) | (row == 6), v1, v2))
        source_stack[half] = jnp.concatenate([m0, m1, m2, squares], axis=0).astype(BF16)

    def split_store(ref, index, block, lanes, value):
        top = value.astype(BF16)
        lanes = slice(lanes, lanes + slots)
        ref[index + (slice(block, block + CHUNK), lanes)] = top
        rest = (value - top.astype(F32)).astype(BF16)
        ref[index + (slice(slots + block, slots + block + CHUNK), lanes)] = rest

    def stage_terms(turn, half):
        slot = slot_of(turn)
        pair_targets = targets_of(turn)
        for side in range(2):
            len_i = table_len[pair_targets[side], 0:1, :]
            fourth = jnp.zeros((8, slots), F32)
            for block in range(0, slots, CHUNK):
                rows = slice(block, block + CHUNK)
                raw = jnp.maximum(dist[half, rows, side * slots : (side + 1) * slots], 1e-30)
                radius = raw * lax.rsqrt(raw)
                t_i = jnp.maximum(len_i - radius, 0.0)
                cube = t_i * t_i * t_i
                t_j = jnp.maximum(columns[half, rows, 48 + side : 49 + side] - radius, 0.0)
                split_store(near_mats, (half,), block, side * slots, cube)
                split_store(far_mats, (slot,), block, side * slots, t_j * t_j * t_j)
                term = cube * t_i * columns[half, rows, 50 + side : 51 + side]
                for at in range(0, CHUNK, 8):
                    fourth = fourth + term[at : at + 8, :]
            for shift in (4, 2, 1):
                fourth = fourth + pltpu.roll(fourth, shift, 0)
            fourths[half, side] = fourth

    def stacked_pieces(value):
        p0, p1, p2 = three_pieces(value)
        stack = jnp.concatenate([p0, p1, p2, jnp.zeros((8, slots), F32)], axis=0).astype(BF16)
        return jnp.concatenate([stack, stack], axis=1)

    def sum_pieces(value):
        return value[0:8, :] + value[8:16, :] + value[16:24, :]

    def target_rows(turn):
        first, second = targets_of(turn)
        return jnp.where(upper, table[first], table[second])

    def moments(first_sums, second_sums, turn):
        sums = jnp.where(upper, first_sums, second_sums)
        weight = jnp.where(upper, first_sums[3:4, :], second_sums[7:8, :])
        return target_rows(turn) * weight - sums

    def stage_sums(turn, half):
        slot = slot_of(turn)
        first, second = targets_of(turn)
        stack = source_stack[half]
        left = jnp.concatenate([stack, stack], axis=1)
        found = dot_plain(left, near_mats[half])

        def piece(at):
            return jnp.where(upper, found[at : at + 8, 0:slots], found[at : at + 8, slots:])

        cubes = piece(0) + piece(8) + piece(16)
        square = piece(24)
        fourth = jnp.where(upper, fourths[half, 0], fourths[half, 1])
        square = square + pltpu.roll(square, 1, 0) + pltpu.roll(square, 2, 0)
        place = jnp.where(upper, table[first], table[second])
        gap = jnp.where(upper, table_gap[first], table_gap[second])
        length = jnp.where(upper, table_len[first], table_len[second])
        weight = jnp.where(upper, cubes[3:4, :], cubes[7:8, :])
        cross = place * cubes
        cross = pltpu.roll(cross, 1, 0) + pltpu.roll(cross, 2, 0) + pltpu.roll(cross, 3, 0)
        dens = gap * weight + 2.0 * cross - square - 0.75 * length * fourth
        slope = place * weight - cubes
        results[pl.ds(slot, 8, stride=stride), :] = jnp.where(weight_row, dens, slope)

    def sums(turn, bank):
        stage_sums(2 * turn, 2 * bank)
        stage_sums(2 * turn + 1, 2 * bank + 1)

    def terms(turn, bank):
        stage_terms(2 * turn, 2 * bank)
        stage_terms(2 * turn + 1, 2 * bank + 1)

    def distances(turn, bank):
        stage_distance(2 * turn, 2 * bank)
        stage_distance(2 * turn + 1, 2 * bank + 1)

    def full_turn(turn, bank):
        for at in range(2):
            stage_terms(2 * turn + at, 2 * bank + at)
            stage_sums(2 * turn - 2 + at, 2 - 2 * bank + at)
            stage_distance(2 * turn + 2 + at, 2 - 2 * bank + at)

    turns = total_count // 2
    mixed = local_count // 2
    local_steps = (mixed - 1) // 2
    early_steps = 1

    def local_step(step, carry):
        full_turn(2 * step + 1, 1)
        full_turn(2 * step + 2, 0)
        return carry

    def far_step(step, carry):
        turn = 2 * step + mixed
        wait_in(step + 1, 4, in_msg, recv_sem)
        full_turn(turn, mixed % 2)
        full_turn(turn + 1, (mixed + 1) % 2)
        return carry

    distances(0, 0)
    terms(0, 0)
    distances(1, 1)
    lax.fori_loop(0, early_steps, local_step, 0)
    pl.semaphore_wait(ready_sem, ring - 1)

    def send(step, carry):
        copy_out(step, out_msg, in_msg, send_sem, recv_sem)
        return carry

    lax.fori_loop(1, peers, send, 0)
    wait_in(0, 1, in_msg, recv_sem)
    lax.fori_loop(early_steps, local_steps, local_step, 0)
    for turn in range(2 * local_steps + 1, mixed):
        full_turn(turn, turn % 2)
    steps = (turns - 1 - mixed) // 2
    lax.fori_loop(0, steps, far_step, 0)
    rest = (peers - 2) % 4
    for turn in range(mixed + 2 * steps, turns - 1):
        wait_in(steps + 1, rest, in_msg, recv_sem)
        full_turn(turn, turn % 2)
    sums(turns - 2, turns % 2)
    terms(turns - 1, (turns - 1) % 2)
    sums(turns - 1, (turns - 1) % 2)

    def summed(quantity):
        parts = []
        for at in (quantity, quantity + 4):
            value = results[at * stride : (at + 1) * stride, :]
            top = value.astype(BF16)
            parts += [top, (value - top.astype(F32)).astype(BF16)]
        return dot_plain(owners, jnp.concatenate(parts, axis=0))

    total = summed(3) * (4.0 * norm)
    safe = jnp.where(occupied, total, 1.0)
    pressure = entropy_ref[...] * jnp.exp(jnp.log(safe) * (-1.0 / 3.0))
    strength = jnp.where(occupied, pressure * (20.0 * norm), 0.0)
    out_ref[0] = jnp.where(occupied, total, 0.0)
    for cell in range(cells):
        table_press[cell] = jnp.broadcast_to(strength[cell : cell + 1, :], (8, slots))

    def send_press(step, carry):
        peer = me ^ step
        chosen = send_s[0, peer]
        first = jnp.where(chosen < 0, cells, chosen)
        second = pair_s[0, peer]
        out_press[step] = jnp.where(row < 1, table_press[first], table_press[second])[0:2, :]
        copy_out(step, out_press, in_press, send_sem2, recv_sem2)
        return carry

    lax.fori_loop(1, peers, send_press, 0, unroll=2)
    near_part = [summed(axis) * strength for axis in range(3)]

    def fill_press(index, first, second):
        in_press[peers + index, 0:1, :] = table_press[first, 0:1, :]
        in_press[peers + index, 1:2, :] = table_press[second, 0:1, :]

    for cell in range(local_next):
        fill_press(cell, cell + 1, cell)
    for turn in range(local_own):
        fill_press(local_next + turn, 2 * turn, 2 * turn + 1)

    def stage_force(turn):
        slot = slot_of(turn)
        press = jnp.where(upper, in_press[slot, 0:1, :], in_press[slot, 1:2, :])
        found = sum_pieces(dot_plain(stacked_pieces(source_rows[slot] * press), far_mats[slot]))
        slope = moments(found[:, 0:slots], found[:, slots : 2 * slots], turn)
        results[pl.ds(slot, 8, stride=stride), :] = slope

    def local_force(step, carry):
        for at in range(11):
            stage_force(11 * step + at)
        return carry

    lax.fori_loop(0, 2, local_force, 0)
    stage_force(22)

    def far_force(step, carry):
        for half in range(4):
            wait_in(4 * step + 1 + half, 4, in_press, recv_sem2)
        for at in range(16):
            stage_force(local_count + 1 + 16 * step + at)
        return carry

    wait_in(0, 1, in_press, recv_sem2)
    stage_force(local_count)
    steps = (peers - 2) // 16
    lax.fori_loop(0, steps, far_force, 0)
    tail = local_count + 1 + 16 * steps
    for at in range(tail, total_count, 4):
        wait_in((at - local_count + 3) // 4, min(4, total_count - at), in_press, recv_sem2)
    for at in range(tail, total_count):
        stage_force(at)
    for axis in range(3):
        out_ref[1 + axis] = jnp.where(occupied, near_part[axis] + summed(axis), 0.0)

    def drain(ref, sem):
        moved = ref.at[pl.ds(0, peers - 1)]
        pltpu.make_async_copy(moved, moved, sem).wait()

    drain(out_msg, send_sem)
    drain(out_press, send_sem2)


def split_kernel(found_ref, density_ref, accel_ref):
    density_ref[...] = found_ref[0]
    accel_ref[...] = found_ref[1:4]


def on_device(send_cells, pair_cell, counts, positions, mass, smooth, entropy):
    cells, slots = mass.shape
    peers = lax.axis_size(("cells", "sub"))
    ring = lax.axis_size("sub")
    chosen = send_cells.reshape(1, peers)
    partner = pair_cell.reshape(1, peers)
    stride = peers + 32
    vmem = pl.BlockSpec(memory_space=pltpu.VMEM)
    smem = pl.BlockSpec(memory_space=pltpu.SMEM)
    found = pl.pallas_call(
        functools.partial(pair_kernel, ring, peers, cells, slots),
        out_shape=jax.ShapeDtypeStruct((4, cells, slots), F32),
        in_specs=[smem, smem, smem] + [vmem] * 6,
        out_specs=vmem,
        scratch_shapes=[
            pltpu.VMEM((cells + 1, 8, slots), F32),
            pltpu.VMEM((cells + 1, 8, slots), F32),
            pltpu.VMEM((cells + 1, 8, slots), F32),
            pltpu.VMEM((cells, 8, slots), F32),
            pltpu.VMEM((4, slots, 64), F32),
            pltpu.VMEM((4, 2, 8, slots), F32),
            pltpu.VMEM((cells, 2, 64, slots), BF16),
            pltpu.VMEM((peers, 10, slots), F32),
            pltpu.VMEM((stride, 10, slots), F32),
            pltpu.VMEM((peers, 2, slots), F32),
            pltpu.VMEM((stride, 2, slots), F32),
            pltpu.VMEM((stride, 8, slots), F32),
            pltpu.VMEM((4, 32, slots), BF16),
            pltpu.VMEM((4, slots, 2 * slots), F32),
            pltpu.VMEM((4, 2 * slots, 2 * slots), BF16),
            pltpu.VMEM((stride, 2 * slots, 2 * slots), BF16),
            pltpu.VMEM((8 * stride, slots), F32),
            pltpu.SemaphoreType.DMA,
            pltpu.SemaphoreType.DMA(((peers + 1) // 4 + 1,)),
            pltpu.SemaphoreType.DMA,
            pltpu.SemaphoreType.DMA(((peers + 1) // 4 + 1,)),
            pltpu.SemaphoreType.REGULAR,
        ],
        compiler_params=pltpu.CompilerParams(
            collective_id=0, has_side_effects=True, vmem_limit_bytes=56 * 2**20
        ),
        name="cell_pairs",
    )(chosen, partner, counts, chosen, partner, positions, mass, smooth, entropy)
    return pl.pallas_call(
        split_kernel,
        out_shape=(
            jax.ShapeDtypeStruct((cells, slots), F32),
            jax.ShapeDtypeStruct((3, cells, slots), F32),
        ),
        in_specs=[vmem],
        out_specs=(vmem, vmem),
        name="split_outputs",
    )(found)


def solution(mesh):
    in_specs = (
        P(("cells", "sub"), None, None),
        P(("cells", "sub"), None, None),
        P(("cells", "sub")),
        P(None, ("cells", "sub"), None),
        P(("cells", "sub"), None),
        P(("cells", "sub"), None),
        P(("cells", "sub"), None),
    )
    out_specs = (P(("cells", "sub"), None), P(None, ("cells", "sub"), None))
    return jax.shard_map(
        on_device, mesh=mesh, in_specs=in_specs, out_specs=out_specs, check_vma=False
    )
```
